32 devices in a mesh: groups: 2 (over x), shard: 16 (over z, y, core).
Axes of the slice: x: 2, y: 2, z: 4, core: 2. Of those that a mesh axis runs over, the one named last changes fastest.
Arguments:
- embeddings: bfloat16 [8192, 1024], P(('groups', 'shard')), parts along dimension 0
- cluster_ids: int32 [8192], P(('groups', 'shard')), parts along dimension 0, may hold values from 0 to 127, as said below
- priority: int32 [8192], P(('groups', 'shard')), parts along dimension 0, may hold values from 0 to 4095, each once
Outputs:
- best_match: float32 [8192], P(('groups', 'shard')), parts along dimension 0
The draws below stay inside these ranges and needn't reach their ends.
There are 2 independent parts, one for each index of `groups`. The reference program is written for one: setup_inputs(seed, part) draws one part's arguments, and reference() takes and returns one part's arrays. A program takes and returns all parts, laid end to end along the dimension named above; each array names one. Nothing has to cross between parts.
Inputs may be any that keep to these rules, and one draw needn't show every extreme that they name: `cluster_ids`: cluster c belongs to owner device c // 8 of the shard axis. The rows of one device hold at most 32 rows of the clusters of any one owner; in every draw one owner receives exactly 32 rows from every device. `priority`: A permutation of the rows of one group.
All inputs are finite; a program needn't handle non-finite values.
Results may differ from the reference program's by a relative error of at most 0.00046.
Values may be sent and summed in bfloat16 or wider, within the bound.
No kernel may reach another device: no remote copies, remote signals or barrier semaphores. Data moves between devices by JAX's collectives and lax.ppermute only.
A program may use at most 64 MiB of HBM per device.

```python
import jax
import jax.numpy as jnp
from jax import lax

D = 1024
ROWS_DEV = 256
CL_DEV = 8
SLOTS = 512
ROWS = 4096
K = 128
N_SHARD = 16


def layout(key):
    capacity = max(2, 2 * ROWS_DEV // N_SHARD)
    slots = N_SHARD * capacity
    full_owner = jax.random.randint(jax.random.fold_in(key, 102), (), 0, N_SHARD)
    base = jnp.arange(slots, dtype=jnp.int32) // capacity

    def device_rows(device_key):
        score = jax.random.permutation(jax.random.fold_in(device_key, 1), slots).astype(jnp.int32)
        score = score + jnp.where(base == full_owner, -slots, 0)
        chosen = base[jnp.argsort(score)[:ROWS_DEV]]
        return jax.random.permutation(jax.random.fold_in(device_key, 2), chosen)
    owner = jax.vmap(device_rows)(jax.random.split(jax.random.fold_in(key, 101), N_SHARD)).reshape(-1)
    steps = jnp.minimum(jnp.arange(CL_DEV, dtype=jnp.int32), 20)
    weights = jnp.maximum(1, 32 // jnp.left_shift(1, steps))
    bounds = jnp.cumsum(weights)
    picks = jax.random.randint(jax.random.fold_in(key, 103), (ROWS,), 0, bounds[-1])
    local = jnp.sum((picks[:, None] >= bounds[None, :]).astype(jnp.int32), axis=1)
    shuffles = jax.vmap(lambda k: jax.random.permutation(k, CL_DEV))(jax.random.split(jax.random.fold_in(key, 104), N_SHARD))
    return (owner * CL_DEV + shuffles[owner, local]).astype(jnp.int32)


def draw_cluster_ids(key, part):
    return layout(key)


def draw_embeddings(key, part):
    clusters = layout(key)
    key = jax.random.fold_in(key, 7)
    centroid = jax.random.normal(jax.random.fold_in(key, 1), (K, D), jnp.float32)
    spread = jnp.exp(jax.random.uniform(jax.random.fold_in(key, 2), (ROWS, 1), jnp.float32, jnp.log(0.15), jnp.log(2.0)))
    scale = jnp.exp(jax.random.uniform(jax.random.fold_in(key, 3), (ROWS, 1), jnp.float32, jnp.log(0.3), jnp.log(3.0)))
    noise = jax.random.normal(jax.random.fold_in(key, 4), (ROWS, D), jnp.float32)
    return ((centroid[clusters] + spread * noise) * scale).astype(jnp.bfloat16)


def setup_inputs(seed: int = 0, part: int = 0) -> dict:
    splits = jax.random.split(jax.random.key(seed), 4)
    own_keys = jax.random.split(jax.random.fold_in(splits[3], part), 4)
    return {
        "embeddings": draw_embeddings(jax.random.fold_in(jax.random.fold_in(splits[3], part), 71), part),
        "cluster_ids": draw_cluster_ids(jax.random.fold_in(jax.random.fold_in(splits[3], part), 71), part),
        "priority": jax.random.permutation(own_keys[2], ROWS).astype(jnp.int32),
    }


def reference(embeddings, cluster_ids, priority):
    wide = embeddings.astype(jnp.float32)
    squares = lax.optimization_barrier(jnp.sum(wide * wide, axis=1, keepdims=True))
    unit = (wide * lax.rsqrt(squares + 1e-06)).astype(jnp.bfloat16)
    first = jnp.argsort(priority, stable=True).astype(jnp.int32)
    order = first[jnp.argsort(cluster_ids[first], stable=True)].astype(jnp.int32)
    sorted_unit = unit[order]
    sorted_cl = cluster_ids[order]
    sorted_rk = priority[order]
    padded_unit = jnp.concatenate([jnp.zeros((SLOTS, D), jnp.bfloat16), sorted_unit], axis=0)
    padded_cl = jnp.concatenate([jnp.full((SLOTS,), -1, jnp.int32), sorted_cl], axis=0)
    padded_rk = jnp.concatenate([jnp.zeros((SLOTS,), jnp.int32), sorted_rk], axis=0)
    block = min(512, ROWS)

    def one_block(index):
        start = (index * block).astype(jnp.int32)
        query = lax.dynamic_slice_in_dim(sorted_unit, start, block, 0)
        query_cl = lax.dynamic_slice_in_dim(sorted_cl, start, block, 0)
        query_rk = lax.dynamic_slice_in_dim(sorted_rk, start, block, 0)
        keys = lax.dynamic_slice_in_dim(padded_unit, start, SLOTS + block, 0)
        keys_cl = lax.dynamic_slice_in_dim(padded_cl, start, SLOTS + block, 0)
        keys_rk = lax.dynamic_slice_in_dim(padded_rk, start, SLOTS + block, 0)
        sims = lax.dot_general(query, keys, (((1,), (1,)), ((), ())), preferred_element_type=jnp.float32)
        mask = (query_cl[:, None] == keys_cl[None, :]) & (keys_rk[None, :] < query_rk[:, None])
        return lax.optimization_barrier(jnp.max(jnp.where(mask, sims, jnp.float32(-1.0)), axis=1))
    result = lax.map(one_block, jnp.arange(ROWS // block, dtype=jnp.int32)).reshape(-1)
    return jnp.zeros((ROWS,), jnp.float32).at[order].set(result)
```

```python
import jax
import jax.numpy as jnp
from jax import lax
from jax.experimental import pallas as pl
from jax.experimental.pallas import tpu as pltpu
from jax.sharding import PartitionSpec as P

CL_DEV = 8
LANES = 128
RADIX = 256
SPAN = 65536


def iota(shape, dim):
    return lax.broadcasted_iota(jnp.int32, shape, dim)


def matmul_nt(left, right):
    return lax.dot_general(
        left, right, (((1,), (1,)), ((), ())), preferred_element_type=jnp.float32
    )


def matmul(left, right):
    return jnp.dot(left, right, preferred_element_type=jnp.float32)


def onehots(mask):
    return jnp.where(mask, 1.0, 0.0).astype(jnp.bfloat16)


def pack_kernel(owners, capacity, emb_ref, cl_ref, rk_ref, out_ref, pos_ref):
    rows, width = emb_ref.shape
    slots = owners * capacity
    cl = cl_ref[...]
    rk = rk_ref[...]
    owner = cl // CL_DEV
    mine = iota((owners, rows), 0) == owner
    earlier = onehots(iota((rows, rows), 0) < iota((rows, rows), 1))
    before = matmul(onehots(mine), earlier)
    pos = jnp.sum(jnp.where(mine, before, 0.0), axis=0, keepdims=True).astype(jnp.int32)
    pos_ref[...] = pos
    place = onehots(iota((slots, rows), 0) == owner * capacity + pos)
    line = iota((LANES, rows), 0)
    meta = jnp.where(
        line == 0,
        cl - owner * CL_DEV + 1,
        jnp.where(line == 1, rk // RADIX, jnp.where(line == 2, rk % RADIX, 0)),
    )
    meta = meta.astype(jnp.float32).astype(jnp.bfloat16)
    out_ref[:, width:] = matmul_nt(place, meta).astype(jnp.bfloat16)
    wide = emb_ref[...].astype(jnp.float32)
    squares = jnp.sum(wide * wide, axis=1, keepdims=True)
    unit = (wide * lax.rsqrt(squares + 1e-06)).astype(jnp.bfloat16)
    out_ref[:, :width] = matmul(place, unit).astype(jnp.bfloat16)


def match_kernel(owners, capacity, in_ref, out_ref):
    slots, full = in_ref.shape
    width = full - LANES
    meta = in_ref[:, width:]
    pick = onehots(iota((8, LANES), 0) == iota((8, LANES), 1))
    across = matmul_nt(pick, meta)
    low = across[0:1] * SPAN
    code = low + across[1:2] * RADIX + across[2:3]
    down = meta.astype(jnp.float32)
    code_down = down[:, 0:1] * SPAN + down[:, 1:2] * RADIX + down[:, 2:3]
    units = in_ref[:, :width]
    best = jnp.full((1, slots), -1.0, jnp.float32)
    step = min(LANES, slots)
    for start in range(0, slots, step):
        sims = matmul_nt(in_ref[start:start + step, :width], units)
        key = code_down[start:start + step]
        seen = jnp.where((key >= low) & (key < code), sims, -1.0)
        best = jnp.maximum(best, jnp.max(seen, axis=0, keepdims=True))
    for source in range(owners):
        base = source * capacity // LANES * LANES
        out_ref[source] = best[:, base:base + LANES]


def unpack_kernel(owners, capacity, got_ref, cl_ref, pos_ref, out_ref):
    rows = cl_ref.shape[1]
    me = lax.axis_index("shard")
    got = got_ref[:, 0, :]
    high = got.astype(jnp.bfloat16)
    rest = got - high.astype(jnp.float32)
    middle = rest.astype(jnp.bfloat16)
    last = (rest - middle.astype(jnp.float32)).astype(jnp.bfloat16)
    lane = pos_ref[...] + lax.rem(me * capacity, LANES)
    pick = onehots(iota((LANES, rows), 0) == lane)
    found = matmul(high, pick) + matmul(middle, pick) + matmul(last, pick)
    mine = iota((owners, rows), 0) == cl_ref[...] // CL_DEV
    out_ref[...] = jnp.sum(jnp.where(mine, found, 0.0), axis=0, keepdims=True)


def call(kernel, shapes, *args):
    return pl.pallas_call(
        kernel,
        out_shape=shapes,
        compiler_params=pltpu.CompilerParams(vmem_limit_bytes=32 * 2**20),
    )(*args)


def shards(embeddings, cluster_ids, priority):
    rows, width = embeddings.shape
    owners = lax.axis_size("shard")
    capacity = max(2, 2 * rows // owners)
    slots = owners * capacity
    cl = cluster_ids.reshape(1, rows)
    rk = priority.reshape(1, rows)
    full = width + LANES

    def pack(*refs):
        pack_kernel(owners, capacity, *refs)

    def match(*refs):
        match_kernel(owners, capacity, *refs)

    def unpack(*refs):
        unpack_kernel(owners, capacity, *refs)

    outgoing, pos = call(
        pack,
        (
            jax.ShapeDtypeStruct((slots, full), jnp.bfloat16),
            jax.ShapeDtypeStruct((1, rows), jnp.int32),
        ),
        embeddings, cl, rk,
    )
    arrived = lax.all_to_all(
        outgoing.reshape(owners, capacity, full), "shard", split_axis=0, concat_axis=0, tiled=True
    ).reshape(slots, full)
    maxima = call(match, jax.ShapeDtypeStruct((owners, 1, LANES), jnp.float32), arrived)
    returned = lax.all_to_all(maxima, "shard", split_axis=0, concat_axis=0, tiled=True)
    out = call(unpack, jax.ShapeDtypeStruct((1, rows), jnp.float32), returned, cl, pos)
    return out.reshape(rows)


def solution(mesh):
    placed = (P(("groups", "shard"), None), P(("groups", "shard")), P(("groups", "shard")))
    return jax.shard_map(
        shards, mesh=mesh, in_specs=placed, out_specs=P(("groups", "shard")), check_vma=False
    )
```

```python
import jax
import jax.numpy as jnp
from jax import lax
from jax.experimental import pallas as pl
from jax.experimental.pallas import tpu as pltpu
from jax.sharding import PartitionSpec as P

CL_DEV = 8
LANES = 128
RADIX = 256
SPAN = 65536


def iota(shape, dim):
    return lax.broadcasted_iota(jnp.int32, shape, dim)


def matmul_nt(left, right):
    return lax.dot_general(
        left, right, (((1,), (1,)), ((), ())), preferred_element_type=jnp.float32
    )


def matmul(left, right):
    return jnp.dot(left, right, preferred_element_type=jnp.float32)


def onehots(mask):
    return jnp.where(mask, 1.0, 0.0).astype(jnp.bfloat16)


def pack_kernel(owners, capacity, paired, emb_any, cl_any, rk_any, *rest):
    *out_refs, pos_ref, emb_ref, cl_ref, rk_ref, sems = rest
    copies = [
        pltpu.make_async_copy(source, target, sems.at[number])
        for number, (source, target) in enumerate(
            ((cl_any, cl_ref), (rk_any, rk_ref), (emb_any, emb_ref))
        )
    ]
    for copy in copies:
        copy.start()
    rows, width = emb_ref.shape
    slots = owners * capacity
    copies[0].wait()
    cl = cl_ref[...]
    owner = cl // CL_DEV
    block = owner ^ lax.axis_index("shard") if paired else owner
    mine = iota((owners, rows), 0) == block
    earlier = onehots(iota((rows, rows), 0) < iota((rows, rows), 1))
    before = matmul(onehots(mine), earlier)
    pos = jnp.sum(jnp.where(mine, before, 0.0), axis=0, keepdims=True).astype(jnp.int32)
    place = block * capacity + pos
    pos_ref[...] = place
    place = onehots(iota((slots, rows), 0) == place)
    copies[1].wait()
    rk = rk_ref[...]
    line = iota((LANES, rows), 0)
    meta = jnp.where(
        line == 0,
        cl - owner * CL_DEV + 1,
        jnp.where(line == 1, rk // RADIX, jnp.where(line == 2, rk % RADIX, 0)),
    )
    meta = matmul_nt(place, meta.astype(jnp.float32).astype(jnp.bfloat16)).astype(jnp.bfloat16)
    copies[2].wait()
    wide = emb_ref[...].astype(jnp.float32)
    squares = jnp.sum(wide * wide, axis=1, keepdims=True)
    unit = (wide * lax.rsqrt(squares + 1e-06)).astype(jnp.bfloat16)
    unit = matmul(place, unit).astype(jnp.bfloat16)
    size = slots // len(out_refs)
    for number, out_ref in enumerate(out_refs):
        out_ref[:, :width] = unit[number * size:(number + 1) * size]
        out_ref[:, width:] = meta[number * size:(number + 1) * size]


def match_kernel(owners, capacity, inputs, *rest):
    in_refs, out_refs = rest[:inputs], rest[inputs:]
    width = in_refs[0].shape[1] - LANES
    slots = owners * capacity
    arrived = jnp.concatenate([ref[...] for ref in in_refs], axis=0)
    meta = arrived[:, width:]
    units = arrived[:, :width]
    pick = onehots(iota((8, LANES), 0) == iota((8, LANES), 1))
    across = matmul_nt(pick, meta)
    low = across[0:1] * SPAN
    code = low + across[1:2] * RADIX + across[2:3]
    down = meta.astype(jnp.float32)
    code_down = down[:, 0:1] * SPAN + down[:, 1:2] * RADIX + down[:, 2:3]
    best = jnp.full((1, slots), -1.0, jnp.float32)
    step = min(LANES, slots)
    for start in range(0, slots, step):
        sims = matmul_nt(units[start:start + step], units)
        key = code_down[start:start + step]
        seen = jnp.where((key >= low) & (key < code), sims, -1.0)
        best = jnp.maximum(best, jnp.max(seen, axis=0, keepdims=True))
    for source in range(owners):
        base = source * capacity // LANES * LANES
        line = best[:, base:base + LANES]
        if len(out_refs) == 1:
            out_refs[0][source] = line
        else:
            out_refs[source][...] = line


def unpack_kernel(owners, capacity, paired, *refs):
    *got_refs, place_ref, out_ref = refs
    rows = place_ref.shape[1]
    place = place_ref[...]
    block = place // capacity
    if paired:
        got = jnp.concatenate([ref[...] for ref in got_refs], axis=0)
        lane = lax.rem(place, LANES)
    else:
        got = got_refs[0][:, 0, :]
        lane = lax.rem(place, capacity) + lax.rem(lax.axis_index("shard") * capacity, LANES)
    high = got.astype(jnp.bfloat16)
    rest = got - high.astype(jnp.float32)
    middle = rest.astype(jnp.bfloat16)
    last = (rest - middle.astype(jnp.float32)).astype(jnp.bfloat16)
    pick = onehots(iota((LANES, rows), 0) == lane)
    found = matmul(high, pick) + matmul(middle, pick) + matmul(last, pick)
    mine = iota((owners, rows), 0) == block
    out_ref[...] = jnp.sum(jnp.where(mine, found, 0.0), axis=0, keepdims=True)


def call(kernel, shapes, args, **kwargs):
    return pl.pallas_call(
        kernel,
        out_shape=shapes,
        compiler_params=pltpu.CompilerParams(vmem_limit_bytes=32 * 2**20),
        **kwargs,
    )(*args)


def exchange(blocks):
    owners = len(blocks)
    return [blocks[0]] + [
        lax.ppermute(blocks[k], "shard", [(d, d ^ k) for d in range(owners)])
        for k in range(1, owners)
    ]


def shards(embeddings, cluster_ids, priority):
    rows, width = embeddings.shape
    owners = lax.axis_size("shard")
    capacity = max(2, 2 * rows // owners)
    slots = owners * capacity
    full = width + LANES
    paired = owners <= 16 and capacity % 16 == 0 and LANES % capacity == 0
    pieces = owners if paired else 1

    def pack(*refs):
        pack_kernel(owners, capacity, paired, *refs)

    def match(*refs):
        match_kernel(owners, capacity, pieces, *refs)

    def unpack(*refs):
        unpack_kernel(owners, capacity, paired, *refs)

    *outgoing, place = call(
        pack,
        [jax.ShapeDtypeStruct((slots // pieces, full), jnp.bfloat16)] * pieces
        + [jax.ShapeDtypeStruct((1, rows), jnp.int32)],
        (embeddings, cluster_ids.reshape(1, rows), priority.reshape(1, rows)),
        in_specs=[pl.BlockSpec(memory_space=pl.ANY)] * 3,
        scratch_shapes=[
            pltpu.VMEM((rows, width), jnp.bfloat16),
            pltpu.VMEM((1, rows), jnp.int32),
            pltpu.VMEM((1, rows), jnp.int32),
            pltpu.SemaphoreType.DMA((3,)),
        ],
    )
    if paired:
        maxima = call(
            match, [jax.ShapeDtypeStruct((1, LANES), jnp.float32)] * owners, exchange(outgoing)
        )
        returned = exchange(maxima)
    else:
        arrived = lax.all_to_all(
            outgoing[0].reshape(owners, capacity, full), "shard", 0, 0, tiled=True
        ).reshape(slots, full)
        maxima = call(match, [jax.ShapeDtypeStruct((owners, 1, LANES), jnp.float32)], [arrived])
        returned = [lax.all_to_all(maxima[0], "shard", 0, 0, tiled=True)]
    out = call(unpack, jax.ShapeDtypeStruct((1, rows), jnp.float32), [*returned, place])
    return out.reshape(rows)


def solution(mesh):
    placed = (P(("groups", "shard"), None), P(("groups", "shard")), P(("groups", "shard")))
    return jax.shard_map(
        shards, mesh=mesh, in_specs=placed, out_specs=P(("groups", "shard")), check_vma=False
    )
```

```python
import jax
import jax.numpy as jnp
from jax import lax
from jax.experimental import pallas as pl
from jax.experimental.pallas import tpu as pltpu
from jax.sharding import PartitionSpec as P

CL_DEV = 8
LANES = 128
RADIX = 256
SPAN = 65536


def iota(shape, dim):
    return lax.broadcasted_iota(jnp.int32, shape, dim)


def matmul_nt(left, right):
    return lax.dot_general(
        left, right, (((1,), (1,)), ((), ())), preferred_element_type=jnp.float32
    )


def matmul(left, right):
    return jnp.dot(left, right, preferred_element_type=jnp.float32)


def onehots(mask):
    return jnp.where(mask, 1.0, 0.0).astype(jnp.bfloat16)


def pack_kernel(owners, capacity, emb_any, cl_any, rk_any, *rest):
    out_ref, place_ref, emb_ref, cl_ref, rk_ref, sems = rest
    copies = [
        pltpu.make_async_copy(source, target, sems.at[number])
        for number, (source, target) in enumerate(
            ((cl_any, cl_ref), (rk_any, rk_ref), (emb_any, emb_ref))
        )
    ]
    for copy in copies:
        copy.start()
    rows, width = emb_ref.shape
    slots = owners * capacity
    copies[0].wait()
    cl = cl_ref[...]
    owner = cl // CL_DEV
    mine = iota((owners, rows), 0) == owner
    earlier = onehots(iota((rows, rows), 0) < iota((rows, rows), 1))
    before = matmul(onehots(mine), earlier)
    pos = jnp.sum(jnp.where(mine, before, 0.0), axis=0, keepdims=True).astype(jnp.int32)
    place = owner * capacity + pos
    place_ref[...] = place
    place = onehots(iota((slots, rows), 0) == place)
    copies[1].wait()
    rk = rk_ref[...]
    line = iota((LANES, rows), 0)
    meta = jnp.where(
        line == 0,
        cl - owner * CL_DEV + 1,
        jnp.where(line == 1, rk // RADIX, jnp.where(line == 2, rk % RADIX, 0)),
    )
    meta = meta.astype(jnp.float32).astype(jnp.bfloat16)
    out_ref[:, width:] = matmul_nt(place, meta).astype(jnp.bfloat16)
    copies[2].wait()
    wide = emb_ref[...].astype(jnp.float32)
    squares = jnp.sum(wide * wide, axis=1, keepdims=True)
    unit = (wide * lax.rsqrt(squares + 1e-06)).astype(jnp.bfloat16)
    out_ref[:, :width] = matmul(place, unit).astype(jnp.bfloat16)


def match_kernel(in_ref, out_ref):
    slots, full = in_ref.shape
    width = full - LANES
    meta = in_ref[:, width:]
    units = in_ref[:, :width]
    pick = onehots(iota((8, LANES), 0) == iota((8, LANES), 1))
    across = matmul_nt(pick, meta)
    low = across[0:1] * SPAN
    code = low + across[1:2] * RADIX + across[2:3]
    down = meta.astype(jnp.float32)
    code_down = down[:, 0:1] * SPAN + down[:, 1:2] * RADIX + down[:, 2:3]
    best = jnp.full((1, slots), -1.0, jnp.float32)
    step = min(LANES, slots)
    for start in range(0, slots, step):
        sims = matmul_nt(units[start:start + step], units)
        key = code_down[start:start + step]
        seen = jnp.where((key >= low) & (key < code), sims, -1.0)
        best = jnp.maximum(best, jnp.max(seen, axis=0, keepdims=True))
    out_ref[0] = best


def unpack_kernel(capacity, got_ref, place_ref, out_ref):
    owners, _, slots = got_ref.shape
    rows = place_ref.shape[1]
    place = place_ref[...]
    got = got_ref[:, 0, :]
    high = got.astype(jnp.bfloat16)
    rest = got - high.astype(jnp.float32)
    middle = rest.astype(jnp.bfloat16)
    last = (rest - middle.astype(jnp.float32)).astype(jnp.bfloat16)
    slot = lax.axis_index("shard") * capacity + lax.rem(place, capacity)
    pick = onehots(iota((slots, rows), 0) == slot)
    found = matmul(high, pick) + matmul(middle, pick) + matmul(last, pick)
    mine = iota((owners, rows), 0) == lax.div(place, capacity)
    out_ref[...] = jnp.sum(jnp.where(mine, found, 0.0), axis=0, keepdims=True)


def call(kernel, shapes, *args, **kwargs):
    return pl.pallas_call(
        kernel,
        out_shape=shapes,
        compiler_params=pltpu.CompilerParams(vmem_limit_bytes=60 * 2**20),
        **kwargs,
    )(*args)


def shards(embeddings, cluster_ids, priority):
    rows, width = embeddings.shape
    owners = lax.axis_size("shard")
    capacity = max(2, 2 * rows // owners)
    slots = owners * capacity
    full = width + LANES

    def pack(*refs):
        pack_kernel(owners, capacity, *refs)

    def unpack(*refs):
        unpack_kernel(capacity, *refs)

    outgoing, place = call(
        pack,
        (
            jax.ShapeDtypeStruct((slots, full), jnp.bfloat16),
            jax.ShapeDtypeStruct((1, rows), jnp.int32),
        ),
        embeddings, cluster_ids.reshape(1, rows), priority.reshape(1, rows),
        in_specs=[pl.BlockSpec(memory_space=pl.ANY)] * 3,
        scratch_shapes=[
            pltpu.VMEM((rows, width), jnp.bfloat16),
            pltpu.VMEM((1, rows), jnp.int32),
            pltpu.VMEM((1, rows), jnp.int32),
            pltpu.SemaphoreType.DMA((3,)),
        ],
    )
    arrived = lax.all_to_all(
        outgoing.reshape(owners, capacity, full), "shard", 0, 0, tiled=True
    ).reshape(slots, full)
    maxima = call(match_kernel, jax.ShapeDtypeStruct((1, 1, slots), jnp.float32), arrived)
    returned = lax.all_gather(maxima, "shard", axis=0, tiled=True)
    out = call(unpack, jax.ShapeDtypeStruct((1, rows), jnp.float32), returned, place)
    return out.reshape(rows)


def solution(mesh):
    placed = (P(("groups", "shard"), None), P(("groups", "shard")), P(("groups", "shard")))
    return jax.shard_map(
        shards, mesh=mesh, in_specs=placed, out_specs=P(("groups", "shard")), check_vma=False
    )
```

```python
import jax
import jax.numpy as jnp
from jax import lax
from jax.experimental import pallas as pl
from jax.experimental.pallas import tpu as pltpu
from jax.sharding import PartitionSpec as P

CL_DEV = 8
LANES = 128
RADIX = 256
SPAN = 65536
META = 16


def iota(shape, dim):
    return lax.broadcasted_iota(jnp.int32, shape, dim)


def matmul_nt(left, right):
    return lax.dot_general(
        left, right, (((1,), (1,)), ((), ())), preferred_element_type=jnp.float32
    )


def matmul(left, right):
    return jnp.dot(left, right, preferred_element_type=jnp.float32)


def onehots(mask):
    return jnp.where(mask, 1.0, 0.0).astype(jnp.bfloat16)


def pack_kernel(owners, capacity, tall, emb_ref, code_ref, out_ref, place_ref):
    rows, width = emb_ref.shape
    slots = owners * capacity
    earlier = onehots(iota((rows, rows), 0) < iota((rows, rows), 1))
    code = code_ref[...]
    cl = lax.div(code, SPAN)
    rk = lax.rem(code, SPAN)
    owner = lax.div(cl, CL_DEV)
    mine = iota((owners, rows), 0) == owner
    before = matmul(onehots(mine), earlier)
    pos = jnp.sum(jnp.where(mine, before, 0.0), axis=0, keepdims=True).astype(jnp.int32)
    place = owner * capacity + pos
    place_ref[...] = place
    place = onehots(iota((slots, rows), 0) == place)
    line = iota((META if tall else LANES, rows), 0)
    meta = jnp.where(
        line == 0,
        cl - owner * CL_DEV + 1,
        jnp.where(line == 1, lax.div(rk, RADIX), jnp.where(line == 2, lax.rem(rk, RADIX), 0)),
    )
    meta = meta.astype(jnp.float32).astype(jnp.bfloat16)
    wide = emb_ref[...].astype(jnp.float32)
    squares = jnp.sum(wide * wide, axis=1, keepdims=True)
    unit = (wide * lax.rsqrt(squares + 1e-06)).astype(jnp.bfloat16)
    unit = matmul(place, unit).astype(jnp.bfloat16)
    if not tall:
        out_ref[:, :width] = unit
        out_ref[:, width:] = matmul_nt(place, meta).astype(jnp.bfloat16)
        return
    meta = matmul_nt(meta, place).astype(jnp.bfloat16)
    pieces = width // LANES
    for target in range(owners):
        top = target * capacity
        for piece in range(pieces):
            out_ref[target, piece * capacity:(piece + 1) * capacity] = unit[
                top:top + capacity, piece * LANES:(piece + 1) * LANES
            ]
        left = top // LANES * LANES
        out_ref[target, pieces * capacity:] = meta[:, left:left + LANES]


def match_kernel(owners, capacity, tall, in_ref, out_ref, *scratch):
    slots = owners * capacity
    if tall:
        units = scratch[0]
        pieces = units.shape[1] // LANES
        for piece in range(pieces):
            units[:, piece * LANES:(piece + 1) * LANES] = in_ref[
                :, piece * capacity:(piece + 1) * capacity
            ].reshape(slots, LANES)
        meta = in_ref[:, pieces * capacity:].reshape(owners * META, LANES)
        left = lax.rem(lax.axis_index("shard") * capacity, LANES)
        shape = (LANES, slots)
        spread = onehots(iota(shape, 0) == left + lax.rem(iota(shape, 1), capacity))
        lines = matmul(meta, spread)
        shape = (owners * META, slots)
        kind = lax.rem(iota(shape, 0), META)
        weight = jnp.where(kind == 0, SPAN, jnp.where(kind == 1, RADIX, jnp.where(kind == 2, 1, 0)))
        own = lax.div(iota(shape, 0), META) == lax.div(iota(shape, 1), capacity)
        code = jnp.where(own, lines * weight.astype(jnp.float32), 0.0)
        code = jnp.sum(code, axis=0, keepdims=True)
        low = code - lax.rem(code.astype(jnp.int32), SPAN).astype(jnp.float32)
        code_down = jnp.broadcast_to(code, (8, slots)).T[:, 0:1]
    else:
        width = in_ref.shape[1] - LANES
        units = in_ref
        meta = in_ref[:, width:]
        pick = onehots(iota((8, LANES), 0) == iota((8, LANES), 1))
        across = matmul_nt(pick, meta)
        low = across[0:1] * SPAN
        code = low + across[1:2] * RADIX + across[2:3]
        down = meta.astype(jnp.float32)
        code_down = down[:, 0:1] * SPAN + down[:, 1:2] * RADIX + down[:, 2:3]
    width = units.shape[1] if tall else width
    best = jnp.full((1, slots), -1.0, jnp.float32)
    step = min(LANES, slots)
    for start in range(0, slots, step):
        sims = matmul_nt(units[start:start + step, :width], units[:, :width])
        key = code_down[start:start + step]
        seen = jnp.where((key >= low) & (key < code), sims, -1.0)
        best = jnp.maximum(best, jnp.max(seen, axis=0, keepdims=True))
    for source in range(owners):
        base = source * capacity // LANES * LANES
        out_ref[source] = best[:, base:base + LANES]


def unpack_kernel(capacity, got_ref, place_ref, out_ref):
    owners = got_ref.shape[0]
    rows = place_ref.shape[1]
    place = place_ref[...]
    got = got_ref[:, 0, :]
    high = got.astype(jnp.bfloat16)
    rest = got - high.astype(jnp.float32)
    middle = rest.astype(jnp.bfloat16)
    last = (rest - middle.astype(jnp.float32)).astype(jnp.bfloat16)
    lane = lax.rem(place, capacity) + lax.rem(lax.axis_index("shard") * capacity, LANES)
    pick = onehots(iota((LANES, rows), 0) == lane)
    found = matmul(high, pick) + matmul(middle, pick) + matmul(last, pick)
    mine = iota((owners, rows), 0) == lax.div(place, capacity)
    out_ref[...] = jnp.sum(jnp.where(mine, found, 0.0), axis=0, keepdims=True)


def call(kernel, shapes, *args, **kwargs):
    return pl.pallas_call(
        kernel,
        out_shape=shapes,
        compiler_params=pltpu.CompilerParams(vmem_limit_bytes=32 * 2**20),
        **kwargs,
    )(*args)


def shards(embeddings, cluster_ids, priority):
    rows, width = embeddings.shape
    owners = lax.axis_size("shard")
    capacity = max(2, 2 * rows // owners)
    slots = owners * capacity
    tall = capacity % 16 == 0 and LANES % capacity == 0
    if tall:
        packed = (owners, width // LANES * capacity + META, LANES)
    else:
        packed = (slots, width + LANES)

    def pack(*refs):
        pack_kernel(owners, capacity, tall, *refs)

    def match(*refs):
        match_kernel(owners, capacity, tall, *refs)

    def unpack(*refs):
        unpack_kernel(capacity, *refs)

    outgoing, place = call(
        pack,
        (
            jax.ShapeDtypeStruct(packed, jnp.bfloat16),
            jax.ShapeDtypeStruct((1, rows), jnp.int32),
        ),
        embeddings, (cluster_ids * SPAN + priority).reshape(1, rows),
    )
    arrived = lax.all_to_all(
        outgoing.reshape(owners, -1, packed[-1]), "shard", 0, 0, tiled=True
    ).reshape(packed)
    maxima = call(
        match,
        jax.ShapeDtypeStruct((owners, 1, LANES), jnp.float32),
        arrived,
        scratch_shapes=[pltpu.VMEM((slots, width), jnp.bfloat16)] if tall else [],
    )
    returned = lax.all_to_all(maxima, "shard", 0, 0, tiled=True)
    out = call(unpack, jax.ShapeDtypeStruct((1, rows), jnp.float32), returned, place)
    return out.reshape(rows)


def solution(mesh):
    placed = (P(("groups", "shard"), None), P(("groups", "shard")), P(("groups", "shard")))
    return jax.shard_map(
        shards, mesh=mesh, in_specs=placed, out_specs=P(("groups", "shard")), check_vma=False
    )
```

```python
import jax
import jax.numpy as jnp
from jax import lax
from jax.experimental import pallas as pl
from jax.experimental.pallas import tpu as pltpu
from jax.sharding import PartitionSpec as P

CL_DEV = 8
LANES = 128
RADIX = 256
SPAN = 65536
META = 16
SPILL = 16


def iota(shape, dim):
    return lax.broadcasted_iota(jnp.int32, shape, dim)


def matmul_nt(left, right):
    return lax.dot_general(
        left, right, (((1,), (1,)), ((), ())), preferred_element_type=jnp.float32
    )


def matmul(left, right):
    return jnp.dot(left, right, preferred_element_type=jnp.float32)


def onehots(mask):
    return jnp.where(mask, 1.0, 0.0).astype(jnp.bfloat16)


def normalised(emb_ref):
    wide = emb_ref[...].astype(jnp.float32)
    squares = jnp.sum(wide * wide, axis=1, keepdims=True)
    return (wide * lax.rsqrt(squares + 1e-06)).astype(jnp.bfloat16)


def positions(owners, code):
    rows = code.shape[1]
    owner = lax.div(code, SPAN * CL_DEV)
    earlier = onehots(iota((rows, rows), 0) < iota((rows, rows), 1))
    mine = iota((owners, rows), 0) == owner
    before = matmul(onehots(mine), earlier)
    pos = jnp.sum(jnp.where(mine, before, 0.0), axis=0, keepdims=True).astype(jnp.int32)
    return owner, pos, earlier


def as_column(row):
    return jnp.broadcast_to(row, (8, row.shape[1])).T[:, 0:1]


def row_base(code):
    return code - lax.rem(code.astype(jnp.int32), SPAN).astype(jnp.float32)


def best_earlier(best, keys, key_code, queries, code, low):
    sims = matmul_nt(keys, queries)
    seen = jnp.where((key_code >= low) & (key_code < code), sims, -1.0)
    return jnp.maximum(best, jnp.max(seen, axis=0, keepdims=True))


def picked(got, pick):
    high = got.astype(jnp.bfloat16)
    rest = got - high.astype(jnp.float32)
    middle = rest.astype(jnp.bfloat16)
    last = (rest - middle.astype(jnp.float32)).astype(jnp.bfloat16)
    return matmul(high, pick) + matmul(middle, pick) + matmul(last, pick)


def pack_all_kernel(owners, capacity, emb_ref, code_ref, out_ref, place_ref):
    rows, width = emb_ref.shape
    code = code_ref[...]
    owner, pos, _ = positions(owners, code)
    place = owner * capacity + pos
    place_ref[...] = place
    place = onehots(iota((owners * capacity, rows), 0) == place)
    cl = lax.div(code, SPAN) - owner * CL_DEV + 1
    rk = lax.rem(code, SPAN)
    line = iota((LANES, rows), 0)
    meta = jnp.where(line == 0, cl, jnp.where(line == 1, lax.div(rk, RADIX), lax.rem(rk, RADIX)))
    meta = jnp.where(line < 3, meta, 0).astype(jnp.float32).astype(jnp.bfloat16)
    out_ref[:, width:] = matmul_nt(place, meta).astype(jnp.bfloat16)
    out_ref[:, :width] = matmul(place, normalised(emb_ref)).astype(jnp.bfloat16)


def match_all_kernel(owners, capacity, in_ref, out_ref):
    slots, full = in_ref.shape
    width = full - LANES
    pick = onehots(iota((8, LANES), 0) == iota((8, LANES), 1))
    across = matmul_nt(pick, in_ref[:, width:])
    code = across[0:1] * SPAN + across[1:2] * RADIX + across[2:3]
    low = row_base(code)
    down = in_ref[:, width:].astype(jnp.float32)
    key_code = down[:, 0:1] * SPAN + down[:, 1:2] * RADIX + down[:, 2:3]
    best = jnp.full((1, slots), -1.0, jnp.float32)
    step = min(LANES, slots)
    for start in range(0, slots, step):
        best = best_earlier(
            best, in_ref[start:start + step, :width], key_code[start:start + step],
            in_ref[:, :width], code, low,
        )
    for source in range(owners):
        base = source * capacity // LANES * LANES
        out_ref[source] = best[:, base:base + LANES]


def unpack_all_kernel(capacity, got_ref, place_ref, out_ref):
    owners = got_ref.shape[0]
    rows = place_ref.shape[1]
    place = place_ref[...]
    lane = lax.rem(place, capacity) + lax.rem(lax.axis_index("shard") * capacity, LANES)
    found = picked(got_ref[:, 0, :], onehots(iota((LANES, rows), 0) == lane))
    mine = iota((owners, rows), 0) == lax.div(place, capacity)
    out_ref[...] = jnp.sum(jnp.where(mine, found, 0.0), axis=0, keepdims=True)


def pack_kernel(owners, tight, capacity, emb_ref, code_ref, out_ref, spill_ref, place_ref):
    rows, width = emb_ref.shape
    code = code_ref[...]
    owner, pos, earlier = positions(owners, code)
    over = pos >= tight
    number = matmul(jnp.broadcast_to(onehots(over), (META, rows)), earlier)[0:1].astype(jnp.int32)
    total = jnp.sum(jnp.where(over, 1.0, 0.0), axis=1, keepdims=True)
    place = jnp.where(over, owners * capacity + number, owner * capacity + pos)
    place_ref[...] = owner * RADIX + jnp.where(over, tight + number, pos)
    cl = lax.div(code, SPAN) + 1
    rk = lax.rem(code, SPAN)
    kinds = (cl, lax.div(rk, RADIX), lax.rem(rk, RADIX))
    line = iota((META, rows), 0)
    groups = owners * capacity // LANES
    meta = jnp.where(iota((META, LANES), 0) == META - 1, total, 0.0)
    for group in range(groups + 1):
        block = jnp.zeros((META, rows), jnp.int32)
        for kind, values in enumerate(kinds):
            at = kind * groups + group if group < groups else groups * len(kinds) + kind
            block = jnp.where(line == at, values, block)
        seats = onehots(iota((LANES, rows), 0) + group * LANES == place)
        meta += matmul_nt(block.astype(jnp.float32).astype(jnp.bfloat16), seats)
    unit = normalised(emb_ref)
    spilt = onehots(iota((SPILL, rows), 0) + owners * capacity == place)
    spilt = matmul(spilt, unit).astype(jnp.bfloat16)
    pieces = width // LANES
    for piece in range(pieces):
        spill_ref[0, piece * SPILL:(piece + 1) * SPILL] = spilt[:, piece * LANES:(piece + 1) * LANES]
    spill_ref[0, pieces * SPILL:] = meta.astype(jnp.bfloat16)
    slot = jnp.where(over, -1, owner * tight + pos)
    out_ref[...] = matmul(
        onehots(iota((owners * tight, rows), 0) == slot), unit
    ).astype(jnp.bfloat16)


def window(source, tight, slots):
    return min(source * tight // LANES * LANES, slots - 2 * LANES)


def match_kernel(owners, tight, capacity, in_ref, spill_ref, out_ref, more_ref, extra):
    slots, width = in_ref.shape
    pieces = width // LANES
    spilt = owners * SPILL
    for piece in range(pieces):
        extra[:, piece * LANES:(piece + 1) * LANES] = spill_ref[
            :, piece * SPILL:(piece + 1) * SPILL
        ].reshape(spilt, LANES)
    meta = spill_ref[:, pieces * SPILL:].reshape(owners * META, LANES)
    lines = owners * META
    kind = lax.rem(iota((lines, 1), 0), META)
    groups = owners * capacity // LANES
    start = lax.axis_index("shard") * capacity
    group = lax.div(start, LANES)
    scales = (SPAN, RADIX, 1)

    def codes(count, at, first):
        shape = (LANES, count * owners)
        seats = onehots(iota(shape, 0) == first + lax.rem(iota(shape, 1), count))
        shape = (lines, count * owners)
        own = lax.div(iota(shape, 0), META) == lax.div(iota(shape, 1), count)
        weight = jnp.zeros((lines, 1), jnp.float32)
        for number, scale in enumerate(scales):
            weight = jnp.where(kind == at(number), float(scale), weight)
        found = jnp.where(own, matmul(meta, seats) * weight, 0.0)
        return jnp.sum(found, axis=0, keepdims=True)

    code = codes(tight, lambda number: number * groups + group, lax.rem(start, LANES))
    code_extra = codes(SPILL, lambda number: groups * len(scales) + number, 0)
    counts = jnp.where(kind == META - 1, meta.astype(jnp.float32), 0.0)
    more_ref[0, 0] = jnp.where(jnp.max(counts) > SPILL, 1, 0)
    low, low_extra = row_base(code), row_base(code_extra)
    best = jnp.full((1, slots), -1.0, jnp.float32)
    best_extra = jnp.full((1, spilt), -1.0, jnp.float32)
    for ref, key_code in ((in_ref, as_column(code)), (extra, as_column(code_extra))):
        for start in range(0, ref.shape[0], LANES):
            keys = ref[start:start + LANES]
            key = key_code[start:start + LANES]
            best = best_earlier(best, keys, key, in_ref[...], code, low)
            best_extra = best_earlier(best_extra, keys, key, extra[...], code_extra, low_extra)
    for source in range(owners):
        base = window(source, tight, slots)
        out_ref[source, :, :2 * LANES] = best[:, base:base + 2 * LANES]
        base = source * SPILL // LANES * LANES
        out_ref[source, :, 2 * LANES:] = best_extra[:, base:base + LANES]


def unpack_kernel(owners, tight, got_ref, place_ref, out_ref):
    rows = place_ref.shape[1]
    me = lax.axis_index("shard")
    place = place_ref[...]
    seat = lax.rem(place, RADIX)
    base = lax.div(me * tight, LANES) * LANES
    base = jnp.minimum(base, owners * tight - 2 * LANES)
    lane = jnp.where(
        seat < tight,
        me * tight - base + seat,
        2 * LANES + lax.rem(me * SPILL, LANES) + seat - tight,
    )
    found = picked(got_ref[:, 0, :], onehots(iota((3 * LANES, rows), 0) == lane))
    mine = iota((owners, rows), 0) == lax.div(place, RADIX)
    out_ref[...] = jnp.sum(jnp.where(mine, found, 0.0), axis=0, keepdims=True)


def call(kernel, shapes, *args, sizes=(), **kwargs):
    def body(*refs):
        kernel(*sizes, *refs)

    return pl.pallas_call(
        body,
        out_shape=shapes,
        compiler_params=pltpu.CompilerParams(vmem_limit_bytes=32 * 2**20),
        **kwargs,
    )(*args)


def exchange(blocks):
    return lax.all_to_all(blocks, "shard", split_axis=0, concat_axis=0, tiled=True)


def with_room_for_all(owners, capacity, embeddings, code):
    rows, width = embeddings.shape
    slots, full = owners * capacity, width + LANES
    seats = jax.ShapeDtypeStruct((1, rows), jnp.int32)
    result = jax.ShapeDtypeStruct((1, rows), jnp.float32)
    packed = jax.ShapeDtypeStruct((slots, full), jnp.bfloat16)
    found = jax.ShapeDtypeStruct((owners, 1, LANES), jnp.float32)
    sizes = (owners, capacity)
    outgoing, place = call(pack_all_kernel, (packed, seats), embeddings, code, sizes=sizes)
    arrived = exchange(outgoing.reshape(owners, capacity, full)).reshape(slots, full)
    maxima = call(match_all_kernel, found, arrived, sizes=sizes)
    return call(unpack_all_kernel, result, exchange(maxima), place, sizes=(capacity,))


def shards(embeddings, cluster_ids, priority):
    rows, width = embeddings.shape
    owners = lax.axis_size("shard")
    capacity = max(2, 2 * rows // owners)
    code = (cluster_ids * SPAN + priority).reshape(1, rows)
    if capacity != 32 or owners != 16:
        return with_room_for_all(owners, capacity, embeddings, code).reshape(rows)
    tight = capacity // 4 * 3
    slots = owners * tight
    height = width // LANES * SPILL + META
    outgoing, spill, place = call(
        pack_kernel,
        (
            jax.ShapeDtypeStruct((slots, width), jnp.bfloat16),
            jax.ShapeDtypeStruct((1, height, LANES), jnp.bfloat16),
            jax.ShapeDtypeStruct((1, rows), jnp.int32),
        ),
        embeddings, code,
        sizes=(owners, tight, capacity),
    )
    spills = lax.all_gather(spill, "shard", axis=0, tiled=True)
    arrived = exchange(outgoing.reshape(owners, tight, width)).reshape(slots, width)
    maxima, more = call(
        match_kernel,
        (
            jax.ShapeDtypeStruct((owners, 1, 3 * LANES), jnp.float32),
            jax.ShapeDtypeStruct((1, 1), jnp.int32),
        ),
        arrived, spills,
        sizes=(owners, tight, capacity),
        out_specs=(
            pl.BlockSpec(memory_space=pltpu.VMEM), pl.BlockSpec(memory_space=pltpu.SMEM)
        ),
        scratch_shapes=[pltpu.VMEM((owners * SPILL, width), jnp.bfloat16)],
    )
    out = call(
        unpack_kernel, jax.ShapeDtypeStruct((1, rows), jnp.float32), exchange(maxima), place,
        sizes=(owners, tight),
    )
    out = lax.cond(
        more[0, 0] > 0,
        lambda: with_room_for_all(owners, capacity, embeddings, code),
        lambda: out,
    )
    return out.reshape(rows)


def solution(mesh):
    placed = (P(("groups", "shard"), None), P(("groups", "shard")), P(("groups", "shard")))
    return jax.shard_map(
        shards, mesh=mesh, in_specs=placed, out_specs=P(("groups", "shard")), check_vma=False
    )
```

```python
import jax
import jax.numpy as jnp
from jax import lax
from jax.experimental import pallas as pl
from jax.experimental.pallas import tpu as pltpu
from jax.sharding import PartitionSpec as P

CL_DEV = 8
LANES = 128
RADIX = 256
SPAN = 65536
META = 8


def iota(shape, dim):
    return lax.broadcasted_iota(jnp.int32, shape, dim)


def matmul_nt(left, right):
    return lax.dot_general(
        left, right, (((1,), (1,)), ((), ())), preferred_element_type=jnp.float32
    )


def matmul(left, right):
    return jnp.dot(left, right, preferred_element_type=jnp.float32)


def onehots(mask):
    return jnp.where(mask, 1.0, 0.0).astype(jnp.bfloat16)


def place_kernel(owners, capacity, tall, code_ref, place_ref, meta_ref):
    rows = code_ref.shape[1]
    code = code_ref[...]
    cl = lax.div(code, SPAN)
    rk = lax.rem(code, SPAN)
    owner = lax.div(cl, CL_DEV)
    mine = iota((owners, rows), 0) == owner
    earlier = onehots(iota((rows, rows), 0) < iota((rows, rows), 1))
    before = matmul(onehots(mine), earlier)
    pos = jnp.sum(jnp.where(mine, before, 0.0), axis=0, keepdims=True).astype(jnp.int32)
    place = owner * capacity + pos
    place_ref[...] = place
    place = onehots(iota((owners * capacity, rows), 0) == place)
    line = iota((META if tall else LANES, rows), 0)
    meta = jnp.where(
        line == 0,
        cl - owner * CL_DEV + 1,
        jnp.where(line == 1, lax.div(rk, RADIX), jnp.where(line == 2, lax.rem(rk, RADIX), 0)),
    )
    meta = meta.astype(jnp.float32).astype(jnp.bfloat16)
    meta_ref[...] = matmul_nt(meta, place) if tall else matmul_nt(place, meta)


def pack_kernel(owners, capacity, tall, emb_ref, place_ref, meta_ref, out_ref):
    rows, width = emb_ref.shape
    place = onehots(iota((owners * capacity, rows), 0) == place_ref[...])
    meta = meta_ref[...].astype(jnp.bfloat16)
    wide = emb_ref[...].astype(jnp.float32)
    squares = jnp.sum(wide * wide, axis=1, keepdims=True)
    unit = (wide * lax.rsqrt(squares + 1e-06)).astype(jnp.bfloat16)
    unit = matmul(place, unit).astype(jnp.bfloat16)
    if not tall:
        out_ref[:, :width] = unit
        out_ref[:, width:] = meta
        return
    pieces = width // LANES
    for target in range(owners):
        top = target * capacity
        for piece in range(pieces):
            out_ref[target, piece * capacity:(piece + 1) * capacity] = unit[
                top:top + capacity, piece * LANES:(piece + 1) * LANES
            ]
        left = top // LANES * LANES
        out_ref[target, pieces * capacity:] = meta[:, left:left + LANES]


def match_kernel(owners, capacity, tall, in_ref, out_ref, *scratch):
    slots = owners * capacity
    if tall:
        units = scratch[0]
        pieces = units.shape[1] // LANES
        for piece in range(pieces):
            units[:, piece * LANES:(piece + 1) * LANES] = in_ref[
                :, piece * capacity:(piece + 1) * capacity
            ].reshape(slots, LANES)
        meta = in_ref[:, pieces * capacity:].reshape(owners * META, LANES)
        left = lax.rem(lax.axis_index("shard") * capacity, LANES)
        shape = (LANES, slots)
        spread = onehots(iota(shape, 0) == left + lax.rem(iota(shape, 1), capacity))
        lines = matmul(meta, spread)
        shape = (owners * META, slots)
        kind = lax.rem(iota(shape, 0), META)
        weight = jnp.where(kind == 0, SPAN, jnp.where(kind == 1, RADIX, jnp.where(kind == 2, 1, 0)))
        own = lax.div(iota(shape, 0), META) == lax.div(iota(shape, 1), capacity)
        code = jnp.where(own, lines * weight.astype(jnp.float32), 0.0)
        code = jnp.sum(code, axis=0, keepdims=True)
        low = code - lax.rem(code.astype(jnp.int32), SPAN).astype(jnp.float32)
        code_down = jnp.broadcast_to(code, (8, slots)).T[:, 0:1]
    else:
        width = in_ref.shape[1] - LANES
        units = in_ref
        meta = in_ref[:, width:]
        pick = onehots(iota((8, LANES), 0) == iota((8, LANES), 1))
        across = matmul_nt(pick, meta)
        low = across[0:1] * SPAN
        code = low + across[1:2] * RADIX + across[2:3]
        down = meta.astype(jnp.float32)
        code_down = down[:, 0:1] * SPAN + down[:, 1:2] * RADIX + down[:, 2:3]
    width = units.shape[1] if tall else width
    step = min(2 * LANES, slots)
    best = []
    for start in range(0, slots, step):
        stop = start + step
        sims = matmul_nt(units[:, :width], units[start:stop, :width])
        seen = (code_down >= low[:, start:stop]) & (code_down < code[:, start:stop])
        best.append(jnp.max(jnp.where(seen, sims, -1.0), axis=0, keepdims=True))
    best = jnp.concatenate(best, axis=1)
    for source in range(owners):
        base = source * capacity // LANES * LANES
        out_ref[source] = best[:, base:base + LANES]


def unpack_kernel(capacity, got_ref, place_ref, out_ref):
    owners = got_ref.shape[0]
    rows = place_ref.shape[1]
    place = place_ref[...]
    got = got_ref[:, 0, :]
    high = got.astype(jnp.bfloat16)
    rest = got - high.astype(jnp.float32)
    middle = rest.astype(jnp.bfloat16)
    last = (rest - middle.astype(jnp.float32)).astype(jnp.bfloat16)
    lane = lax.rem(place, capacity) + lax.rem(lax.axis_index("shard") * capacity, LANES)
    pick = onehots(iota((LANES, rows), 0) == lane)
    found = matmul(high, pick) + matmul(middle, pick) + matmul(last, pick)
    mine = iota((owners, rows), 0) == lax.div(place, capacity)
    out_ref[...] = jnp.sum(jnp.where(mine, found, 0.0), axis=0, keepdims=True)


def call(kernel, shapes, *args, **kwargs):
    return pl.pallas_call(
        kernel,
        out_shape=shapes,
        compiler_params=pltpu.CompilerParams(vmem_limit_bytes=32 * 2**20),
        **kwargs,
    )(*args)


def shards(embeddings, cluster_ids, priority):
    rows, width = embeddings.shape
    owners = lax.axis_size("shard")
    capacity = max(2, 2 * rows // owners)
    slots = owners * capacity
    tall = capacity % 16 == 0 and LANES % capacity == 0
    if tall:
        packed = (owners, width // LANES * capacity + META, LANES)
    else:
        packed = (slots, width + LANES)

    def find(*refs):
        place_kernel(owners, capacity, tall, *refs)

    def pack(*refs):
        pack_kernel(owners, capacity, tall, *refs)

    def match(*refs):
        match_kernel(owners, capacity, tall, *refs)

    def unpack(*refs):
        unpack_kernel(capacity, *refs)

    place, meta = call(
        find,
        (
            jax.ShapeDtypeStruct((1, rows), jnp.int32),
            jax.ShapeDtypeStruct((META, slots) if tall else (slots, LANES), jnp.float32),
        ),
        (cluster_ids * SPAN + priority).reshape(1, rows),
        cost_estimate=pl.CostEstimate(
            flops=300_000_000, bytes_accessed=100_000, transcendentals=0
        ),
    )
    outgoing = call(
        pack, jax.ShapeDtypeStruct(packed, jnp.bfloat16), embeddings, place, meta
    )
    arrived = lax.all_to_all(
        outgoing.reshape(owners, -1, packed[-1]), "shard", 0, 0, tiled=True
    ).reshape(packed)
    maxima = call(
        match,
        jax.ShapeDtypeStruct((owners, 1, LANES), jnp.float32),
        arrived,
        scratch_shapes=[pltpu.VMEM((slots, width), jnp.bfloat16)] if tall else [],
    )
    returned = lax.all_to_all(maxima, "shard", 0, 0, tiled=True)
    out = call(unpack, jax.ShapeDtypeStruct((1, rows), jnp.float32), returned, place)
    return out.reshape(rows)


def solution(mesh):
    placed = (P(("groups", "shard"), None), P(("groups", "shard")), P(("groups", "shard")))
    return jax.shard_map(
        shards, mesh=mesh, in_specs=placed, out_specs=P(("groups", "shard")), check_vma=False
    )
```

```python
import jax
import jax.numpy as jnp
from jax import lax
from jax.experimental import pallas as pl
from jax.experimental.pallas import tpu as pltpu
from jax.sharding import PartitionSpec as P

CL_DEV = 8
LANES = 128
RADIX = 256
SPAN = 65536
META = 8


def iota(shape, dim):
    return lax.broadcasted_iota(jnp.int32, shape, dim)


def matmul_nt(left, right):
    return lax.dot_general(
        left, right, (((1,), (1,)), ((), ())), preferred_element_type=jnp.float32
    )


def matmul(left, right):
    return jnp.dot(left, right, preferred_element_type=jnp.float32)


def onehots(mask):
    return jnp.where(mask, 1.0, 0.0).astype(jnp.bfloat16)


def block_order(owners):
    half = owners // 2
    far = list(range(half, owners))
    near = list(range(half - 1, -1, -1))
    order = far[:2]
    for block in far[2:]:
        order += [block, near.pop(0)]
    return order + near


def place_kernel(owners, capacity, paired, code_ref, place_ref, meta_ref):
    rows = code_ref.shape[1]
    code = code_ref[...]
    cl = lax.div(code, SPAN)
    rk = lax.rem(code, SPAN)
    owner = lax.div(cl, CL_DEV)
    block = owner ^ lax.axis_index("shard") if paired else owner
    mine = iota((owners, rows), 0) == block
    earlier = onehots(iota((rows, rows), 0) < iota((rows, rows), 1))
    before = matmul(onehots(mine), earlier)
    pos = jnp.sum(jnp.where(mine, before, 0.0), axis=0, keepdims=True).astype(jnp.int32)
    place = block * capacity + pos
    place_ref[...] = place
    place = onehots(iota((owners * capacity, rows), 0) == place)
    line = iota((META if paired else LANES, rows), 0)
    meta = jnp.where(
        line == 0,
        cl - owner * CL_DEV + 1,
        jnp.where(line == 1, lax.div(rk, RADIX), jnp.where(line == 2, lax.rem(rk, RADIX), 0)),
    )
    meta = meta.astype(jnp.float32).astype(jnp.bfloat16)
    meta_ref[...] = matmul_nt(meta, place) if paired else matmul_nt(place, meta)


def pack_kernel(owners, capacity, paired, emb_ref, place_ref, meta_ref, *out_refs):
    rows, width = emb_ref.shape
    place = onehots(iota((owners * capacity, rows), 0) == place_ref[...])
    meta = meta_ref[...].astype(jnp.bfloat16)
    wide = emb_ref[...].astype(jnp.float32)
    squares = jnp.sum(wide * wide, axis=1, keepdims=True)
    unit = (wide * lax.rsqrt(squares + 1e-06)).astype(jnp.bfloat16)
    unit = matmul(place, unit).astype(jnp.bfloat16)
    if not paired:
        out_refs[0][:, :width] = unit
        out_refs[0][:, width:] = meta
        return
    pieces = width // LANES
    for block, out_ref in zip(block_order(owners), out_refs):
        top = block * capacity
        for piece in range(pieces):
            out_ref[piece * capacity:(piece + 1) * capacity] = unit[
                top:top + capacity, piece * LANES:(piece + 1) * LANES
            ]
        left = top // LANES * LANES
        out_ref[pieces * capacity:] = meta[:, left:left + LANES]


def maxima(units, code, code_down):
    slots = code.shape[1]
    low = code - lax.rem(code.astype(jnp.int32), SPAN).astype(jnp.float32)
    step = min(2 * LANES, slots)
    best = []
    for start in range(0, slots, step):
        stop = start + step
        sims = matmul_nt(units(0, slots), units(start, stop))
        seen = (code_down >= low[:, start:stop]) & (code_down < code[:, start:stop])
        best.append(jnp.max(jnp.where(seen, sims, -1.0), axis=0, keepdims=True))
    return jnp.concatenate(best, axis=1)


def match_paired_kernel(owners, capacity, *refs):
    *in_refs, out_ref, rows_ref = refs
    in_refs = dict(zip(block_order(owners), in_refs))
    slots, width = rows_ref.shape
    pieces = width // LANES
    for block, in_ref in in_refs.items():
        top = block * capacity
        for piece in range(pieces):
            rows_ref[top:top + capacity, piece * LANES:(piece + 1) * LANES] = in_ref[
                piece * capacity:(piece + 1) * capacity
            ]
    each = LANES // capacity
    part = lax.div(iota((META, LANES), 1), capacity)
    code = []
    for first in range(0, owners, each):
        meta = jnp.zeros((META, LANES), jnp.float32)
        for number in range(each):
            lines = in_refs[first + number][pieces * capacity:].astype(jnp.float32)
            meta = jnp.where(part == number, lines, meta)
        code.append(meta[0:1] * SPAN + meta[1:2] * RADIX + meta[2:3])
    code = jnp.concatenate(code, axis=1)
    code_down = jnp.broadcast_to(code, (8, slots)).T[:, 0:1]
    best = maxima(lambda start, stop: rows_ref[start:stop], code, code_down)
    me = lax.axis_index("shard")
    for block in range(owners):
        base = block * capacity // LANES * LANES
        out_ref[me ^ block] = best[:, base:base + LANES]


def match_kernel(owners, capacity, in_ref, out_ref):
    width = in_ref.shape[1] - LANES
    meta = in_ref[:, width:]
    pick = onehots(iota((8, LANES), 0) == iota((8, LANES), 1))
    across = matmul_nt(pick, meta)
    code = across[0:1] * SPAN + across[1:2] * RADIX + across[2:3]
    down = meta.astype(jnp.float32)
    code_down = down[:, 0:1] * SPAN + down[:, 1:2] * RADIX + down[:, 2:3]
    best = maxima(lambda start, stop: in_ref[start:stop, :width], code, code_down)
    for source in range(owners):
        base = source * capacity // LANES * LANES
        out_ref[source] = best[:, base:base + LANES]


def unpack_kernel(capacity, paired, got_ref, place_ref, out_ref):
    owners = got_ref.shape[0]
    rows = place_ref.shape[1]
    me = lax.axis_index("shard")
    place = place_ref[...]
    owner = lax.div(place, capacity)
    if paired:
        owner = owner ^ me
        lane = lax.rem(place, LANES)
    else:
        lane = lax.rem(place, capacity) + lax.rem(me * capacity, LANES)
    got = got_ref[:, 0, :]
    high = got.astype(jnp.bfloat16)
    rest = got - high.astype(jnp.float32)
    middle = rest.astype(jnp.bfloat16)
    last = (rest - middle.astype(jnp.float32)).astype(jnp.bfloat16)
    pick = onehots(iota((LANES, rows), 0) == lane)
    found = matmul(high, pick) + matmul(middle, pick) + matmul(last, pick)
    mine = iota((owners, rows), 0) == owner
    out_ref[...] = jnp.sum(jnp.where(mine, found, 0.0), axis=0, keepdims=True)


def call(kernel, sizes, shapes, *args, **kwargs):
    def body(*refs):
        kernel(*sizes, *refs)

    return pl.pallas_call(
        body,
        out_shape=shapes,
        compiler_params=pltpu.CompilerParams(vmem_limit_bytes=32 * 2**20),
        **kwargs,
    )(*args)


def swap(blocks):
    owners = len(blocks)
    return [
        lax.ppermute(block, "shard", [(d, d ^ k) for d in range(owners)]) if k else block
        for k, block in zip(block_order(owners), blocks)
    ]


def shards(embeddings, cluster_ids, priority):
    rows, width = embeddings.shape
    owners = lax.axis_size("shard")
    capacity = max(2, 2 * rows // owners)
    slots = owners * capacity
    paired = owners == 16 and capacity % 16 == 0 and LANES % capacity == 0
    sizes = (owners, capacity, paired)
    place, meta = call(
        place_kernel,
        sizes,
        (
            jax.ShapeDtypeStruct((1, rows), jnp.int32),
            jax.ShapeDtypeStruct((META, slots) if paired else (slots, LANES), jnp.float32),
        ),
        (cluster_ids * SPAN + priority).reshape(1, rows),
        cost_estimate=pl.CostEstimate(
            flops=300_000_000, bytes_accessed=100_000, transcendentals=0
        ),
    )
    found = jax.ShapeDtypeStruct((owners, 1, LANES), jnp.float32)
    if paired:
        block = jax.ShapeDtypeStruct((width // LANES * capacity + META, LANES), jnp.bfloat16)
        outgoing = call(pack_kernel, sizes, [block] * owners, embeddings, place, meta)
        best = call(
            match_paired_kernel,
            (owners, capacity),
            found,
            *swap(outgoing),
            scratch_shapes=[pltpu.VMEM((slots, width), jnp.bfloat16)],
        )
    else:
        full = width + LANES
        packed = jax.ShapeDtypeStruct((slots, full), jnp.bfloat16)
        (outgoing,) = call(pack_kernel, sizes, [packed], embeddings, place, meta)
        arrived = lax.all_to_all(
            outgoing.reshape(owners, capacity, full), "shard", 0, 0, tiled=True
        ).reshape(slots, full)
        best = call(match_kernel, (owners, capacity), found, arrived)
    returned = lax.all_to_all(best, "shard", 0, 0, tiled=True)
    out = call(
        unpack_kernel,
        (capacity, paired),
        jax.ShapeDtypeStruct((1, rows), jnp.float32),
        returned,
        place,
    )
    return out.reshape(rows)


def solution(mesh):
    placed = (P(("groups", "shard"), None), P(("groups", "shard")), P(("groups", "shard")))
    return jax.shard_map(
        shards, mesh=mesh, in_specs=placed, out_specs=P(("groups", "shard")), check_vma=False
    )
```

```python
import jax
import jax.numpy as jnp
from jax import lax
from jax.experimental import pallas as pl
from jax.experimental.pallas import tpu as pltpu
from jax.sharding import PartitionSpec as P

CL_DEV = 8
LANES = 128
RADIX = 256
SPAN = 65536
META = 8


def iota(shape, dim):
    return lax.broadcasted_iota(jnp.int32, shape, dim)


def matmul_nt(left, right):
    return lax.dot_general(
        left, right, (((1,), (1,)), ((), ())), preferred_element_type=jnp.float32
    )


def matmul(left, right):
    return jnp.dot(left, right, preferred_element_type=jnp.float32)


def onehots(mask):
    return jnp.where(mask, 1.0, 0.0).astype(jnp.bfloat16)


def pair_order(owners):
    half = owners // 2
    return list(range(half, owners, 2)) + list(range(0, half, 2))


def swap_steps(owners):
    return [
        (8, None), (10, None), (2, None), (4, None), (12, None),
        (9, 8), (6, 2), (14, 9), (3, 4), (11, 10), (5, 3), (7, 6), (1, 11), (13, 12), (15, 14),
    ]


def swapped_order(owners):
    return [block for block, _ in swap_steps(owners)] + [0]


def place_kernel(owners, capacity, paired, code_ref, place_ref, meta_ref):
    rows = code_ref.shape[1]
    code = code_ref[...]
    cl = lax.div(code, SPAN)
    rk = lax.rem(code, SPAN)
    owner = lax.div(cl, CL_DEV)
    block = owner ^ lax.axis_index("shard") if paired else owner
    mine = iota((owners, rows), 0) == block
    earlier = onehots(iota((rows, rows), 0) < iota((rows, rows), 1))
    before = matmul(onehots(mine), earlier)
    pos = jnp.sum(jnp.where(mine, before, 0.0), axis=0, keepdims=True).astype(jnp.int32)
    place = block * capacity + pos
    place_ref[...] = place
    place = onehots(iota((owners * capacity, rows), 0) == place)
    line = iota((META if paired else LANES, rows), 0)
    meta = jnp.where(
        line == 0,
        cl - owner * CL_DEV + 1,
        jnp.where(line == 1, lax.div(rk, RADIX), jnp.where(line == 2, lax.rem(rk, RADIX), 0)),
    )
    meta = meta.astype(jnp.float32).astype(jnp.bfloat16)
    meta_ref[...] = matmul_nt(meta, place) if paired else matmul_nt(place, meta)


def pack_kernel(owners, capacity, paired, emb_ref, place_ref, meta_ref, *out_refs):
    rows, width = emb_ref.shape
    place = onehots(iota((owners * capacity, rows), 0) == place_ref[...])
    meta = meta_ref[...].astype(jnp.bfloat16)
    wide = emb_ref[...].astype(jnp.float32)
    squares = jnp.sum(wide * wide, axis=1, keepdims=True)
    unit = (wide * lax.rsqrt(squares + 1e-06)).astype(jnp.bfloat16)
    unit = matmul(place, unit).astype(jnp.bfloat16)
    if not paired:
        out_refs[0][:, :width] = unit
        out_refs[0][:, width:] = meta
        return
    pieces = width // LANES
    for first, out_ref in zip(pair_order(owners), out_refs):
        for piece in range(2 * pieces):
            top = (first + piece // pieces) * capacity
            left = piece % pieces * LANES
            out_ref[piece * capacity:(piece + 1) * capacity] = unit[
                top:top + capacity, left:left + LANES
            ]
        left = first * capacity // LANES * LANES
        out_ref[2 * pieces * capacity:] = meta[:, left:left + LANES]


def maxima(units, code, code_down):
    slots = code.shape[1]
    low = code - lax.rem(code.astype(jnp.int32), SPAN).astype(jnp.float32)
    step = min(2 * LANES, slots)
    best = []
    for start in range(0, slots, step):
        stop = start + step
        sims = matmul_nt(units(0, slots), units(start, stop))
        seen = (code_down >= low[:, start:stop]) & (code_down < code[:, start:stop])
        best.append(jnp.max(jnp.where(seen, sims, -1.0), axis=0, keepdims=True))
    return jnp.concatenate(best, axis=1)


def match_paired_kernel(owners, capacity, *refs):
    *in_refs, out_ref, rows_ref = refs
    in_refs = dict(zip(swapped_order(owners), in_refs))
    slots, width = rows_ref.shape
    pieces = width // LANES
    for block, in_ref in in_refs.items():
        top = block * capacity
        base = block % 2 * pieces
        for piece in range(pieces):
            start = (base + piece) * capacity
            rows_ref[top:top + capacity, piece * LANES:(piece + 1) * LANES] = in_ref[
                start:start + capacity
            ]
    each = LANES // capacity
    part = lax.div(iota((META, LANES), 1), capacity)
    code = []
    for first in range(0, owners, each):
        meta = jnp.zeros((META, LANES), jnp.float32)
        for number in range(each):
            lines = in_refs[first + number][2 * pieces * capacity:].astype(jnp.float32)
            meta = jnp.where(part == number, lines, meta)
        code.append(meta[0:1] * SPAN + meta[1:2] * RADIX + meta[2:3])
    code = jnp.concatenate(code, axis=1)
    code_down = jnp.broadcast_to(code, (8, slots)).T[:, 0:1]
    best = maxima(lambda start, stop: rows_ref[start:stop], code, code_down)
    me = lax.axis_index("shard")
    for block in range(owners):
        base = block * capacity // LANES * LANES
        out_ref[me ^ block] = best[:, base:base + LANES]


def match_kernel(owners, capacity, in_ref, out_ref):
    width = in_ref.shape[1] - LANES
    meta = in_ref[:, width:]
    pick = onehots(iota((8, LANES), 0) == iota((8, LANES), 1))
    across = matmul_nt(pick, meta)
    code = across[0:1] * SPAN + across[1:2] * RADIX + across[2:3]
    down = meta.astype(jnp.float32)
    code_down = down[:, 0:1] * SPAN + down[:, 1:2] * RADIX + down[:, 2:3]
    best = maxima(lambda start, stop: in_ref[start:stop, :width], code, code_down)
    for source in range(owners):
        base = source * capacity // LANES * LANES
        out_ref[source] = best[:, base:base + LANES]


def unpack_kernel(capacity, paired, got_ref, place_ref, out_ref):
    owners = got_ref.shape[0]
    rows = place_ref.shape[1]
    me = lax.axis_index("shard")
    place = place_ref[...]
    owner = lax.div(place, capacity)
    if paired:
        owner = owner ^ me
        lane = lax.rem(place, LANES)
    else:
        lane = lax.rem(place, capacity) + lax.rem(me * capacity, LANES)
    got = got_ref[:, 0, :]
    high = got.astype(jnp.bfloat16)
    rest = got - high.astype(jnp.float32)
    middle = rest.astype(jnp.bfloat16)
    last = (rest - middle.astype(jnp.float32)).astype(jnp.bfloat16)
    pick = onehots(iota((LANES, rows), 0) == lane)
    found = matmul(high, pick) + matmul(middle, pick) + matmul(last, pick)
    mine = iota((owners, rows), 0) == owner
    out_ref[...] = jnp.sum(jnp.where(mine, found, 0.0), axis=0, keepdims=True)


def call(kernel, sizes, shapes, *args, **kwargs):
    def body(*refs):
        kernel(*sizes, *refs)

    return pl.pallas_call(
        body,
        out_shape=shapes,
        compiler_params=pltpu.CompilerParams(vmem_limit_bytes=32 * 2**20),
        **kwargs,
    )(*args)


def swap(pairs, owners):
    got = dict(zip(pair_order(owners), pairs))
    sent = dict(got)

    def across(pair, k):
        return lax.ppermute(pair, "shard", [(d, d ^ k) for d in range(owners)])

    def after(value, other):
        return lax.optimization_barrier((value, other))

    for step in swap_steps(owners):
        block, wait = step
        first = block - block % 2
        pair = got[first] if block % 2 else sent[first]
        if wait is not None:
            pair, got[wait] = after(pair, got[wait])
        got[block] = across(pair, 1 if block % 2 else block)
    return [got[block] for block in swapped_order(owners)]


def shards(embeddings, cluster_ids, priority):
    rows, width = embeddings.shape
    owners = lax.axis_size("shard")
    capacity = max(2, 2 * rows // owners)
    slots = owners * capacity
    paired = owners == 16 and capacity % 16 == 0 and LANES % capacity == 0
    sizes = (owners, capacity, paired)
    place, meta = call(
        place_kernel,
        sizes,
        (
            jax.ShapeDtypeStruct((1, rows), jnp.int32),
            jax.ShapeDtypeStruct((META, slots) if paired else (slots, LANES), jnp.float32),
        ),
        (cluster_ids * SPAN + priority).reshape(1, rows),
        cost_estimate=pl.CostEstimate(
            flops=300_000_000, bytes_accessed=100_000, transcendentals=0
        ),
    )
    found = jax.ShapeDtypeStruct((owners, 1, LANES), jnp.float32)
    if paired:
        height = 2 * (width // LANES) * capacity + META
        pair = jax.ShapeDtypeStruct((height, LANES), jnp.bfloat16)
        outgoing = call(pack_kernel, sizes, [pair] * (owners // 2), embeddings, place, meta)
        best = call(
            match_paired_kernel,
            (owners, capacity),
            found,
            *swap(outgoing, owners),
            scratch_shapes=[pltpu.VMEM((slots, width), jnp.bfloat16)],
        )
    else:
        full = width + LANES
        packed = jax.ShapeDtypeStruct((slots, full), jnp.bfloat16)
        (outgoing,) = call(pack_kernel, sizes, [packed], embeddings, place, meta)
        arrived = lax.all_to_all(
            outgoing.reshape(owners, capacity, full), "shard", 0, 0, tiled=True
        ).reshape(slots, full)
        best = call(match_kernel, (owners, capacity), found, arrived)
    returned = lax.all_to_all(best, "shard", 0, 0, tiled=True)
    out = call(
        unpack_kernel,
        (capacity, paired),
        jax.ShapeDtypeStruct((1, rows), jnp.float32),
        returned,
        place,
    )
    return out.reshape(rows)


def solution(mesh):
    placed = (P(("groups", "shard"), None), P(("groups", "shard")), P(("groups", "shard")))
    return jax.shard_map(
        shards, mesh=mesh, in_specs=placed, out_specs=P(("groups", "shard")), check_vma=False
    )
```

```python
import jax
import jax.numpy as jnp
from jax import lax
from jax.experimental import pallas as pl
from jax.experimental.pallas import tpu as pltpu
from jax.sharding import PartitionSpec as P

CL_DEV = 8
LANES = 128
RADIX = 256
SPAN = 65536
META = 8


def iota(shape, dim):
    return lax.broadcasted_iota(jnp.int32, shape, dim)


def matmul_nt(left, right):
    return lax.dot_general(
        left, right, (((1,), (1,)), ((), ())), preferred_element_type=jnp.float32
    )


def matmul(left, right):
    return jnp.dot(left, right, preferred_element_type=jnp.float32)


def onehots(mask):
    return jnp.where(mask, 1.0, 0.0).astype(jnp.bfloat16)


def place_kernel(owners, capacity, paired, code_ref, place_ref, meta_ref):
    rows = code_ref.shape[1]
    code = code_ref[...]
    cl = lax.div(code, SPAN)
    rk = lax.rem(code, SPAN)
    owner = lax.div(cl, CL_DEV)
    block = owner ^ lax.axis_index("shard") if paired else owner
    mine = iota((owners, rows), 0) == block
    earlier = onehots(iota((rows, rows), 0) < iota((rows, rows), 1))
    before = matmul(onehots(mine), earlier)
    pos = jnp.sum(jnp.where(mine, before, 0.0), axis=0, keepdims=True).astype(jnp.int32)
    place = block * capacity + pos
    place_ref[...] = place
    place = onehots(iota((owners * capacity, rows), 0) == place)
    line = iota((META if paired else LANES, rows), 0)
    meta = jnp.where(
        line == 0,
        cl - owner * CL_DEV + 1,
        jnp.where(line == 1, lax.div(rk, RADIX), jnp.where(line == 2, lax.rem(rk, RADIX), 0)),
    )
    meta = meta.astype(jnp.float32).astype(jnp.bfloat16)
    meta_ref[...] = matmul_nt(meta, place) if paired else matmul_nt(place, meta)


def pack_kernel(owners, capacity, paired, emb_ref, place_ref, meta_ref, *out_refs):
    rows, width = emb_ref.shape
    place = onehots(iota((owners * capacity, rows), 0) == place_ref[...])
    meta = meta_ref[...].astype(jnp.bfloat16)
    wide = emb_ref[...].astype(jnp.float32)
    squares = jnp.sum(wide * wide, axis=1, keepdims=True)
    unit = (wide * lax.rsqrt(squares + 1e-06)).astype(jnp.bfloat16)
    unit = matmul(place, unit).astype(jnp.bfloat16)
    if not paired:
        out_refs[0][:, :width] = unit
        out_refs[0][:, width:] = meta
        return
    pieces = width // LANES
    half = owners // 2
    me = lax.rem(lax.axis_index("shard"), half)
    *pair_refs, near_ref = out_refs
    for block in range(owners):
        if block < half:
            out_ref, base = near_ref.at[me ^ block], 0
        else:
            out_ref, base = pair_refs[(block - half) // 2], block % 2 * pieces * capacity
        top = block * capacity
        for piece in range(pieces):
            start = base + piece * capacity
            out_ref[start:start + capacity] = unit[
                top:top + capacity, piece * LANES:(piece + 1) * LANES
            ]
        if block < half or block % 2 == 0:
            left = top // LANES * LANES
            out_ref[out_ref.shape[0] - META:] = meta[:, left:left + LANES]


def maxima(units, code, code_down):
    slots = code.shape[1]
    low = code - lax.rem(code.astype(jnp.int32), SPAN).astype(jnp.float32)
    step = min(2 * LANES, slots)
    best = []
    for start in range(0, slots, step):
        stop = start + step
        sims = matmul_nt(units(0, slots), units(start, stop))
        seen = (code_down >= low[:, start:stop]) & (code_down < code[:, start:stop])
        best.append(jnp.max(jnp.where(seen, sims, -1.0), axis=0, keepdims=True))
    return jnp.concatenate(best, axis=1)


def match_paired_kernel(owners, capacity, *refs):
    *pair_refs, near_ref, out_ref, rows_ref = refs
    half = owners // 2
    me = lax.axis_index("shard")
    slots, width = rows_ref.shape
    pieces = width // LANES
    in_refs = [near_ref.at[lax.rem(me, half) ^ block] for block in range(half)] + pair_refs
    for block, in_ref in enumerate(in_refs):
        top = block * capacity
        base = block % 2 * pieces if block >= half else 0
        for piece in range(pieces):
            start = (base + piece) * capacity
            rows_ref[top:top + capacity, piece * LANES:(piece + 1) * LANES] = in_ref[
                start:start + capacity
            ]
    each = LANES // capacity
    part = lax.div(iota((META, LANES), 1), capacity)
    code = []
    for first in range(0, owners, each):
        meta = jnp.zeros((META, LANES), jnp.float32)
        for number in range(each):
            in_ref = in_refs[first + number]
            lines = in_ref[in_ref.shape[0] - META:].astype(jnp.float32)
            meta = jnp.where(part == number, lines, meta)
        code.append(meta[0:1] * SPAN + meta[1:2] * RADIX + meta[2:3])
    code = jnp.concatenate(code, axis=1)
    code_down = jnp.broadcast_to(code, (8, slots)).T[:, 0:1]
    best = maxima(lambda start, stop: rows_ref[start:stop], code, code_down)
    for block in range(owners):
        base = block * capacity // LANES * LANES
        out_ref[me ^ block] = best[:, base:base + LANES]


def match_kernel(owners, capacity, in_ref, out_ref):
    width = in_ref.shape[1] - LANES
    meta = in_ref[:, width:]
    pick = onehots(iota((8, LANES), 0) == iota((8, LANES), 1))
    across = matmul_nt(pick, meta)
    code = across[0:1] * SPAN + across[1:2] * RADIX + across[2:3]
    down = meta.astype(jnp.float32)
    code_down = down[:, 0:1] * SPAN + down[:, 1:2] * RADIX + down[:, 2:3]
    best = maxima(lambda start, stop: in_ref[start:stop, :width], code, code_down)
    for source in range(owners):
        base = source * capacity // LANES * LANES
        out_ref[source] = best[:, base:base + LANES]


def unpack_kernel(capacity, paired, got_ref, place_ref, out_ref):
    owners = got_ref.shape[0]
    rows = place_ref.shape[1]
    me = lax.axis_index("shard")
    place = place_ref[...]
    owner = lax.div(place, capacity)
    if paired:
        owner = owner ^ me
        lane = lax.rem(place, LANES)
    else:
        lane = lax.rem(place, capacity) + lax.rem(me * capacity, LANES)
    got = got_ref[:, 0, :]
    high = got.astype(jnp.bfloat16)
    rest = got - high.astype(jnp.float32)
    middle = rest.astype(jnp.bfloat16)
    last = (rest - middle.astype(jnp.float32)).astype(jnp.bfloat16)
    pick = onehots(iota((LANES, rows), 0) == lane)
    found = matmul(high, pick) + matmul(middle, pick) + matmul(last, pick)
    mine = iota((owners, rows), 0) == owner
    out_ref[...] = jnp.sum(jnp.where(mine, found, 0.0), axis=0, keepdims=True)


def call(kernel, sizes, shapes, *args, **kwargs):
    def body(*refs):
        kernel(*sizes, *refs)

    return pl.pallas_call(
        body,
        out_shape=shapes,
        compiler_params=pltpu.CompilerParams(vmem_limit_bytes=32 * 2**20),
        **kwargs,
    )(*args)


def swap(pairs, near, owners):
    half = owners // 2

    def across(value, distance):
        return lax.ppermute(value, "shard", [(d, d ^ distance) for d in range(owners)])

    far = [across(pair, half + 2 * number) for number, pair in enumerate(pairs)]
    groups = [list(range(half)), list(range(half, owners))]
    near = lax.all_to_all(near, "shard", 0, 0, axis_index_groups=groups, tiled=True)
    far[0], near = lax.optimization_barrier((far[0], near))
    got = []
    for pair in far:
        got += [pair, across(pair, 1)]
    return [*got, near]


def shards(embeddings, cluster_ids, priority):
    rows, width = embeddings.shape
    owners = lax.axis_size("shard")
    capacity = max(2, 2 * rows // owners)
    slots = owners * capacity
    paired = owners == 16 and capacity % 16 == 0 and LANES % capacity == 0
    sizes = (owners, capacity, paired)
    place, meta = call(
        place_kernel,
        sizes,
        (
            jax.ShapeDtypeStruct((1, rows), jnp.int32),
            jax.ShapeDtypeStruct((META, slots) if paired else (slots, LANES), jnp.float32),
        ),
        (cluster_ids * SPAN + priority).reshape(1, rows),
        cost_estimate=pl.CostEstimate(
            flops=300_000_000, bytes_accessed=100_000, transcendentals=0
        ),
    )
    found = jax.ShapeDtypeStruct((owners, 1, LANES), jnp.float32)
    if paired:
        height = width // LANES * capacity
        half = owners // 2
        *pairs, near = call(
            pack_kernel,
            sizes,
            [jax.ShapeDtypeStruct((2 * height + META, LANES), jnp.bfloat16)] * (half // 2)
            + [jax.ShapeDtypeStruct((half, height + META, LANES), jnp.bfloat16)],
            embeddings, place, meta,
        )
        best = call(
            match_paired_kernel,
            (owners, capacity),
            found,
            *swap(pairs, near, owners),
            scratch_shapes=[pltpu.VMEM((slots, width), jnp.bfloat16)],
        )
    else:
        full = width + LANES
        packed = jax.ShapeDtypeStruct((slots, full), jnp.bfloat16)
        (outgoing,) = call(pack_kernel, sizes, [packed], embeddings, place, meta)
        arrived = lax.all_to_all(
            outgoing.reshape(owners, capacity, full), "shard", 0, 0, tiled=True
        ).reshape(slots, full)
        best = call(match_kernel, (owners, capacity), found, arrived)
    returned = lax.all_to_all(best, "shard", 0, 0, tiled=True)
    out = call(
        unpack_kernel,
        (capacity, paired),
        jax.ShapeDtypeStruct((1, rows), jnp.float32),
        returned,
        place,
    )
    return out.reshape(rows)


def solution(mesh):
    placed = (P(("groups", "shard"), None), P(("groups", "shard")), P(("groups", "shard")))
    return jax.shard_map(
        shards, mesh=mesh, in_specs=placed, out_specs=P(("groups", "shard")), check_vma=False
    )
```

```python
import jax
import jax.numpy as jnp
from jax import lax
from jax.experimental import pallas as pl
from jax.experimental.pallas import tpu as pltpu
from jax.sharding import PartitionSpec as P

CL_DEV = 8
LANES = 128
RADIX = 256
SPAN = 65536
META = 8


def iota(shape, dim):
    return lax.broadcasted_iota(jnp.int32, shape, dim)


def matmul_nt(left, right):
    return lax.dot_general(
        left, right, (((1,), (1,)), ((), ())), preferred_element_type=jnp.float32
    )


def matmul(left, right):
    return jnp.dot(left, right, preferred_element_type=jnp.float32)


def onehots(mask):
    return jnp.where(mask, 1.0, 0.0).astype(jnp.bfloat16)


def block_order(owners):
    half = owners // 2
    quarter = half // 2
    far = [half + part * quarter + k for k in range(quarter) for part in range(2)]
    near = list(range(half - 1, -1, -1))
    order = far[:2]
    for block in far[2:half - 2]:
        order += [near.pop(0), block]
    return order + [far[-2], near.pop(0), far[-1]] + near


def place_kernel(owners, capacity, paired, code_ref, place_ref, meta_ref):
    rows = code_ref.shape[1]
    code = code_ref[...]
    cl = lax.div(code, SPAN)
    rk = lax.rem(code, SPAN)
    owner = lax.div(cl, CL_DEV)
    block = owner ^ lax.axis_index("shard") if paired else owner
    mine = iota((owners, rows), 0) == block
    earlier = onehots(iota((rows, rows), 0) < iota((rows, rows), 1))
    before = matmul(onehots(mine), earlier)
    pos = jnp.sum(jnp.where(mine, before, 0.0), axis=0, keepdims=True).astype(jnp.int32)
    place = block * capacity + pos
    place_ref[...] = place
    place = onehots(iota((owners * capacity, rows), 0) == place)
    line = iota((META if paired else LANES, rows), 0)
    meta = jnp.where(
        line == 0,
        cl - owner * CL_DEV + 1,
        jnp.where(line == 1, lax.div(rk, RADIX), jnp.where(line == 2, lax.rem(rk, RADIX), 0)),
    )
    meta = meta.astype(jnp.float32).astype(jnp.bfloat16)
    meta_ref[...] = matmul_nt(meta, place) if paired else matmul_nt(place, meta)


def pack_kernel(owners, capacity, paired, emb_ref, place_ref, meta_ref, *out_refs):
    rows, width = emb_ref.shape
    place = onehots(iota((owners * capacity, rows), 0) == place_ref[...])
    meta = meta_ref[...].astype(jnp.bfloat16)
    wide = emb_ref[...].astype(jnp.float32)
    squares = jnp.sum(wide * wide, axis=1, keepdims=True)
    unit = (wide * lax.rsqrt(squares + 1e-06)).astype(jnp.bfloat16)
    unit = matmul(place, unit).astype(jnp.bfloat16)
    if not paired:
        out_refs[0][:, :width] = unit
        out_refs[0][:, width:] = meta
        return
    pieces = width // LANES
    for block, out_ref in zip(block_order(owners), out_refs):
        top = block * capacity
        for piece in range(pieces):
            out_ref[piece * capacity:(piece + 1) * capacity] = unit[
                top:top + capacity, piece * LANES:(piece + 1) * LANES
            ]
        left = top // LANES * LANES
        out_ref[pieces * capacity:] = meta[:, left:left + LANES]


def maxima(units, code, code_down):
    slots = code.shape[1]
    low = code - lax.rem(code.astype(jnp.int32), SPAN).astype(jnp.float32)
    step = min(2 * LANES, slots)
    best = []
    for start in range(0, slots, step):
        stop = start + step
        sims = matmul_nt(units(0, slots), units(start, stop))
        seen = (code_down >= low[:, start:stop]) & (code_down < code[:, start:stop])
        best.append(jnp.max(jnp.where(seen, sims, -1.0), axis=0, keepdims=True))
    return jnp.concatenate(best, axis=1)


def match_paired_kernel(owners, capacity, *refs):
    *in_refs, out_ref, rows_ref = refs
    in_refs = dict(zip(block_order(owners), in_refs))
    slots, width = rows_ref.shape
    pieces = width // LANES
    for block, in_ref in in_refs.items():
        top = block * capacity
        for piece in range(pieces):
            rows_ref[top:top + capacity, piece * LANES:(piece + 1) * LANES] = in_ref[
                piece * capacity:(piece + 1) * capacity
            ]
    each = LANES // capacity
    part = lax.div(iota((META, LANES), 1), capacity)
    code = []
    for first in range(0, owners, each):
        meta = jnp.zeros((META, LANES), jnp.float32)
        for number in range(each):
            lines = in_refs[first + number][pieces * capacity:].astype(jnp.float32)
            meta = jnp.where(part == number, lines, meta)
        code.append(meta[0:1] * SPAN + meta[1:2] * RADIX + meta[2:3])
    code = jnp.concatenate(code, axis=1)
    code_down = jnp.broadcast_to(code, (8, slots)).T[:, 0:1]
    best = maxima(lambda start, stop: rows_ref[start:stop], code, code_down)
    me = lax.axis_index("shard")
    for block in range(owners):
        base = block * capacity // LANES * LANES
        out_ref[me ^ block] = best[:, base:base + LANES]


def match_kernel(owners, capacity, in_ref, out_ref):
    width = in_ref.shape[1] - LANES
    meta = in_ref[:, width:]
    pick = onehots(iota((8, LANES), 0) == iota((8, LANES), 1))
    across = matmul_nt(pick, meta)
    code = across[0:1] * SPAN + across[1:2] * RADIX + across[2:3]
    down = meta.astype(jnp.float32)
    code_down = down[:, 0:1] * SPAN + down[:, 1:2] * RADIX + down[:, 2:3]
    best = maxima(lambda start, stop: in_ref[start:stop, :width], code, code_down)
    for source in range(owners):
        base = source * capacity // LANES * LANES
        out_ref[source] = best[:, base:base + LANES]


def unpack_kernel(capacity, paired, got_ref, place_ref, out_ref):
    owners = got_ref.shape[0]
    rows = place_ref.shape[1]
    me = lax.axis_index("shard")
    place = place_ref[...]
    owner = lax.div(place, capacity)
    if paired:
        owner = owner ^ me
        lane = lax.rem(place, LANES)
    else:
        lane = lax.rem(place, capacity) + lax.rem(me * capacity, LANES)
    got = got_ref[:, 0, :]
    high = got.astype(jnp.bfloat16)
    rest = got - high.astype(jnp.float32)
    middle = rest.astype(jnp.bfloat16)
    last = (rest - middle.astype(jnp.float32)).astype(jnp.bfloat16)
    pick = onehots(iota((LANES, rows), 0) == lane)
    found = matmul(high, pick) + matmul(middle, pick) + matmul(last, pick)
    mine = iota((owners, rows), 0) == owner
    out_ref[...] = jnp.sum(jnp.where(mine, found, 0.0), axis=0, keepdims=True)


def call(kernel, sizes, shapes, *args, **kwargs):
    def body(*refs):
        kernel(*sizes, *refs)

    return pl.pallas_call(
        body,
        out_shape=shapes,
        compiler_params=pltpu.CompilerParams(vmem_limit_bytes=32 * 2**20),
        **kwargs,
    )(*args)


def swap(blocks):
    owners = len(blocks)
    return [
        lax.ppermute(block, "shard", [(d, d ^ k) for d in range(owners)]) if k else block
        for k, block in zip(block_order(owners), blocks)
    ]


def shards(embeddings, cluster_ids, priority):
    rows, width = embeddings.shape
    owners = lax.axis_size("shard")
    capacity = max(2, 2 * rows // owners)
    slots = owners * capacity
    paired = owners == 16 and capacity % 16 == 0 and LANES % capacity == 0
    sizes = (owners, capacity, paired)
    place, meta = call(
        place_kernel,
        sizes,
        (
            jax.ShapeDtypeStruct((1, rows), jnp.int32),
            jax.ShapeDtypeStruct((META, slots) if paired else (slots, LANES), jnp.float32),
        ),
        (cluster_ids * SPAN + priority).reshape(1, rows),
        cost_estimate=pl.CostEstimate(
            flops=300_000_000, bytes_accessed=100_000, transcendentals=0
        ),
    )
    found = jax.ShapeDtypeStruct((owners, 1, LANES), jnp.float32)
    if paired:
        block = jax.ShapeDtypeStruct((width // LANES * capacity + META, LANES), jnp.bfloat16)
        outgoing = call(pack_kernel, sizes, [block] * owners, embeddings, place, meta)
        best = call(
            match_paired_kernel,
            (owners, capacity),
            found,
            *swap(outgoing),
            scratch_shapes=[pltpu.VMEM((slots, width), jnp.bfloat16)],
        )
    else:
        full = width + LANES
        packed = jax.ShapeDtypeStruct((slots, full), jnp.bfloat16)
        (outgoing,) = call(pack_kernel, sizes, [packed], embeddings, place, meta)
        arrived = lax.all_to_all(
            outgoing.reshape(owners, capacity, full), "shard", 0, 0, tiled=True
        ).reshape(slots, full)
        best = call(match_kernel, (owners, capacity), found, arrived)
    returned = lax.all_to_all(best, "shard", 0, 0, tiled=True)
    out = call(
        unpack_kernel,
        (capacity, paired),
        jax.ShapeDtypeStruct((1, rows), jnp.float32),
        returned,
        place,
    )
    return out.reshape(rows)


def solution(mesh):
    placed = (P(("groups", "shard"), None), P(("groups", "shard")), P(("groups", "shard")))
    return jax.shard_map(
        shards, mesh=mesh, in_specs=placed, out_specs=P(("groups", "shard")), check_vma=False
    )
```

```python
import jax
import jax.numpy as jnp
from jax import lax
from jax.experimental import pallas as pl
from jax.experimental.pallas import tpu as pltpu
from jax.sharding import PartitionSpec as P

CL_DEV = 8
LANES = 128
RADIX = 256
SPAN = 65536
META = 8


def iota(shape, dim):
    return lax.broadcasted_iota(jnp.int32, shape, dim)


def matmul_nt(left, right):
    return lax.dot_general(
        left, right, (((1,), (1,)), ((), ())), preferred_element_type=jnp.float32
    )


def matmul(left, right):
    return jnp.dot(left, right, preferred_element_type=jnp.float32)


def onehots(mask):
    return jnp.where(mask, 1.0, 0.0).astype(jnp.bfloat16)


def block_order(owners):
    half = owners // 2
    quarter = half // 2
    far = [half + part * quarter + k for k in range(quarter) for part in range(2)]
    near = list(range(half - 1, -1, -1))
    order = far[:2]
    for place in range(2, owners):
        crosses = place in (2, 4, 6, 7, 9, 11)
        order.append(far[sum(block >= half for block in order)] if crosses else near.pop(0))
    return order


def place_kernel(owners, capacity, paired, code_ref, place_ref, meta_ref):
    rows = code_ref.shape[1]
    code = code_ref[...]
    cl = lax.div(code, SPAN)
    rk = lax.rem(code, SPAN)
    owner = lax.div(cl, CL_DEV)
    block = owner ^ lax.axis_index("shard") if paired else owner
    mine = iota((owners, rows), 0) == block
    earlier = onehots(iota((rows, rows), 0) < iota((rows, rows), 1))
    before = matmul(onehots(mine), earlier)
    pos = jnp.sum(jnp.where(mine, before, 0.0), axis=0, keepdims=True).astype(jnp.int32)
    place = block * capacity + pos
    place_ref[...] = place
    place = onehots(iota((owners * capacity, rows), 0) == place)
    line = iota((META if paired else LANES, rows), 0)
    meta = jnp.where(
        line == 0,
        cl - owner * CL_DEV + 1,
        jnp.where(line == 1, lax.div(rk, RADIX), jnp.where(line == 2, lax.rem(rk, RADIX), 0)),
    )
    meta = meta.astype(jnp.float32).astype(jnp.bfloat16)
    meta_ref[...] = matmul_nt(meta, place) if paired else matmul_nt(place, meta)


def pack_kernel(owners, capacity, paired, emb_ref, place_ref, meta_ref, *out_refs):
    rows, width = emb_ref.shape
    place = onehots(iota((owners * capacity, rows), 0) == place_ref[...])
    meta = meta_ref[...].astype(jnp.bfloat16)
    wide = emb_ref[...].astype(jnp.float32)
    squares = jnp.sum(wide * wide, axis=1, keepdims=True)
    unit = (wide * lax.rsqrt(squares + 1e-06)).astype(jnp.bfloat16)
    unit = matmul(place, unit).astype(jnp.bfloat16)
    if not paired:
        out_refs[0][:, :width] = unit
        out_refs[0][:, width:] = meta
        return
    pieces = width // LANES
    for block, out_ref in zip(block_order(owners), out_refs):
        top = block * capacity
        for piece in range(pieces):
            out_ref[piece * capacity:(piece + 1) * capacity] = unit[
                top:top + capacity, piece * LANES:(piece + 1) * LANES
            ]
        left = top // LANES * LANES
        out_ref[pieces * capacity:] = meta[:, left:left + LANES]


def maxima(units, code, code_down):
    slots = code.shape[1]
    low = code - lax.rem(code.astype(jnp.int32), SPAN).astype(jnp.float32)
    step = min(2 * LANES, slots)
    best = []
    for start in range(0, slots, step):
        stop = start + step
        sims = matmul_nt(units(0, slots), units(start, stop))
        seen = (code_down >= low[:, start:stop]) & (code_down < code[:, start:stop])
        best.append(jnp.max(jnp.where(seen, sims, -1.0), axis=0, keepdims=True))
    return jnp.concatenate(best, axis=1)


def match_paired_kernel(owners, capacity, *refs):
    *in_refs, out_ref, rows_ref = refs
    in_refs = dict(zip(block_order(owners), in_refs))
    slots, width = rows_ref.shape
    pieces = width // LANES
    for block, in_ref in in_refs.items():
        top = block * capacity
        for piece in range(pieces):
            rows_ref[top:top + capacity, piece * LANES:(piece + 1) * LANES] = in_ref[
                piece * capacity:(piece + 1) * capacity
            ]
    each = LANES // capacity
    part = lax.div(iota((META, LANES), 1), capacity)
    code = []
    for first in range(0, owners, each):
        meta = jnp.zeros((META, LANES), jnp.float32)
        for number in range(each):
            lines = in_refs[first + number][pieces * capacity:].astype(jnp.float32)
            meta = jnp.where(part == number, lines, meta)
        code.append(meta[0:1] * SPAN + meta[1:2] * RADIX + meta[2:3])
    code = jnp.concatenate(code, axis=1)
    code_down = jnp.broadcast_to(code, (8, slots)).T[:, 0:1]
    best = maxima(lambda start, stop: rows_ref[start:stop], code, code_down)
    me = lax.axis_index("shard")
    for block in range(owners):
        base = block * capacity // LANES * LANES
        out_ref[me ^ block] = best[:, base:base + LANES]


def match_kernel(owners, capacity, in_ref, out_ref):
    width = in_ref.shape[1] - LANES
    meta = in_ref[:, width:]
    pick = onehots(iota((8, LANES), 0) == iota((8, LANES), 1))
    across = matmul_nt(pick, meta)
    code = across[0:1] * SPAN + across[1:2] * RADIX + across[2:3]
    down = meta.astype(jnp.float32)
    code_down = down[:, 0:1] * SPAN + down[:, 1:2] * RADIX + down[:, 2:3]
    best = maxima(lambda start, stop: in_ref[start:stop, :width], code, code_down)
    for source in range(owners):
        base = source * capacity // LANES * LANES
        out_ref[source] = best[:, base:base + LANES]


def unpack_kernel(capacity, paired, got_ref, place_ref, out_ref):
    owners = got_ref.shape[0]
    rows = place_ref.shape[1]
    me = lax.axis_index("shard")
    place = place_ref[...]
    owner = lax.div(place, capacity)
    if paired:
        owner = owner ^ me
        lane = lax.rem(place, LANES)
    else:
        lane = lax.rem(place, capacity) + lax.rem(me * capacity, LANES)
    got = got_ref[:, 0, :]
    high = got.astype(jnp.bfloat16)
    rest = got - high.astype(jnp.float32)
    middle = rest.astype(jnp.bfloat16)
    last = (rest - middle.astype(jnp.float32)).astype(jnp.bfloat16)
    pick = onehots(iota((LANES, rows), 0) == lane)
    found = matmul(high, pick) + matmul(middle, pick) + matmul(last, pick)
    mine = iota((owners, rows), 0) == owner
    out_ref[...] = jnp.sum(jnp.where(mine, found, 0.0), axis=0, keepdims=True)


def call(kernel, sizes, shapes, *args, **kwargs):
    def body(*refs):
        kernel(*sizes, *refs)

    return pl.pallas_call(
        body,
        out_shape=shapes,
        compiler_params=pltpu.CompilerParams(vmem_limit_bytes=32 * 2**20),
        **kwargs,
    )(*args)


def swap(blocks):
    owners = len(blocks)
    return [
        lax.ppermute(block, "shard", [(d, d ^ k) for d in range(owners)]) if k else block
        for k, block in zip(block_order(owners), blocks)
    ]


def shards(embeddings, cluster_ids, priority):
    rows, width = embeddings.shape
    owners = lax.axis_size("shard")
    capacity = max(2, 2 * rows // owners)
    slots = owners * capacity
    paired = owners == 16 and capacity % 16 == 0 and LANES % capacity == 0
    sizes = (owners, capacity, paired)
    place, meta = call(
        place_kernel,
        sizes,
        (
            jax.ShapeDtypeStruct((1, rows), jnp.int32),
            jax.ShapeDtypeStruct((META, slots) if paired else (slots, LANES), jnp.float32),
        ),
        (cluster_ids * SPAN + priority).reshape(1, rows),
        cost_estimate=pl.CostEstimate(
            flops=300_000_000, bytes_accessed=100_000, transcendentals=0
        ),
    )
    found = jax.ShapeDtypeStruct((owners, 1, LANES), jnp.float32)
    if paired:
        block = jax.ShapeDtypeStruct((width // LANES * capacity + META, LANES), jnp.bfloat16)
        outgoing = call(pack_kernel, sizes, [block] * owners, embeddings, place, meta)
        best = call(
            match_paired_kernel,
            (owners, capacity),
            found,
            *swap(outgoing),
            scratch_shapes=[pltpu.VMEM((slots, width), jnp.bfloat16)],
        )
    else:
        full = width + LANES
        packed = jax.ShapeDtypeStruct((slots, full), jnp.bfloat16)
        (outgoing,) = call(pack_kernel, sizes, [packed], embeddings, place, meta)
        arrived = lax.all_to_all(
            outgoing.reshape(owners, capacity, full), "shard", 0, 0, tiled=True
        ).reshape(slots, full)
        best = call(match_kernel, (owners, capacity), found, arrived)
    returned = lax.all_to_all(best, "shard", 0, 0, tiled=True)
    out = call(
        unpack_kernel,
        (capacity, paired),
        jax.ShapeDtypeStruct((1, rows), jnp.float32),
        returned,
        place,
    )
    return out.reshape(rows)


def solution(mesh):
    placed = (P(("groups", "shard"), None), P(("groups", "shard")), P(("groups", "shard")))
    return jax.shard_map(
        shards, mesh=mesh, in_specs=placed, out_specs=P(("groups", "shard")), check_vma=False
    )
```

```python
import jax
import jax.numpy as jnp
from jax import lax
from jax.experimental import pallas as pl
from jax.experimental.pallas import tpu as pltpu
from jax.sharding import PartitionSpec as P

CL_DEV = 8
LANES = 128
RADIX = 256
SPAN = 65536
META = 8


def iota(shape, dim):
    return lax.broadcasted_iota(jnp.int32, shape, dim)


def matmul_nt(left, right):
    return lax.dot_general(
        left, right, (((1,), (1,)), ((), ())), preferred_element_type=jnp.float32
    )


def matmul(left, right):
    return jnp.dot(left, right, preferred_element_type=jnp.float32)


def onehots(mask):
    return jnp.where(mask, 1.0, 0.0).astype(jnp.bfloat16)


def block_order(owners):
    half = owners // 2
    quarter = half // 2
    far = [half + part * quarter + k for k in range(quarter) for part in range(2)]
    near = list(range(half - 1, -1, -1))
    order = far[:2]
    for block in far[2:]:
        order += [near.pop(0), block]
    return order + near


def place_kernel(owners, capacity, paired, code_ref, place_ref, meta_ref):
    rows = code_ref.shape[1]
    code = code_ref[...]
    cl = lax.div(code, SPAN)
    rk = lax.rem(code, SPAN)
    owner = lax.div(cl, CL_DEV)
    block = owner ^ lax.axis_index("shard") if paired else owner
    mine = iota((owners, rows), 0) == block
    earlier = onehots(iota((rows, rows), 0) < iota((rows, rows), 1))
    before = matmul(onehots(mine), earlier)
    pos = jnp.sum(jnp.where(mine, before, 0.0), axis=0, keepdims=True).astype(jnp.int32)
    place = block * capacity + pos
    place_ref[...] = place
    place = onehots(iota((owners * capacity, rows), 0) == place)
    line = iota((META if paired else LANES, rows), 0)
    meta = jnp.where(
        line == 0,
        cl - owner * CL_DEV + 1,
        jnp.where(line == 1, lax.div(rk, RADIX), jnp.where(line == 2, lax.rem(rk, RADIX), 0)),
    )
    meta = meta.astype(jnp.float32).astype(jnp.bfloat16)
    meta_ref[...] = matmul_nt(meta, place) if paired else matmul_nt(place, meta)


def pack_kernel(owners, capacity, paired, emb_ref, place_ref, meta_ref, *out_refs):
    rows, width = emb_ref.shape
    place = onehots(iota((owners * capacity, rows), 0) == place_ref[...])
    meta = meta_ref[...].astype(jnp.bfloat16)
    wide = emb_ref[...].astype(jnp.float32)
    squares = jnp.sum(wide * wide, axis=1, keepdims=True)
    unit = (wide * lax.rsqrt(squares + 1e-06)).astype(jnp.bfloat16)
    unit = matmul(place, unit).astype(jnp.bfloat16)
    if not paired:
        out_refs[0][:, :width] = unit
        out_refs[0][:, width:] = meta
        return
    pieces = width // LANES
    for block, out_ref in zip(block_order(owners), out_refs):
        top = block * capacity
        for piece in range(pieces):
            out_ref[piece * capacity:(piece + 1) * capacity] = unit[
                top:top + capacity, piece * LANES:(piece + 1) * LANES
            ]
        left = top // LANES * LANES
        out_ref[pieces * capacity:] = meta[:, left:left + LANES]


def maxima(units, code, code_down):
    slots = code.shape[1]
    low = code - lax.rem(code.astype(jnp.int32), SPAN).astype(jnp.float32)
    step = min(2 * LANES, slots)
    best = []
    for start in range(0, slots, step):
        stop = start + step
        sims = matmul_nt(units(0, slots), units(start, stop))
        seen = (code_down >= low[:, start:stop]) & (code_down < code[:, start:stop])
        best.append(jnp.max(jnp.where(seen, sims, -1.0), axis=0, keepdims=True))
    return jnp.concatenate(best, axis=1)


def match_paired_kernel(owners, capacity, *refs):
    *in_refs, out_ref, rows_ref = refs
    in_refs = dict(zip(block_order(owners), in_refs))
    slots, width = rows_ref.shape
    pieces = width // LANES
    for block, in_ref in in_refs.items():
        top = block * capacity
        for piece in range(pieces):
            rows_ref[top:top + capacity, piece * LANES:(piece + 1) * LANES] = in_ref[
                piece * capacity:(piece + 1) * capacity
            ]
    each = LANES // capacity
    part = lax.div(iota((META, LANES), 1), capacity)
    code = []
    for first in range(0, owners, each):
        meta = jnp.zeros((META, LANES), jnp.float32)
        for number in range(each):
            lines = in_refs[first + number][pieces * capacity:].astype(jnp.float32)
            meta = jnp.where(part == number, lines, meta)
        code.append(meta[0:1] * SPAN + meta[1:2] * RADIX + meta[2:3])
    code = jnp.concatenate(code, axis=1)
    code_down = jnp.broadcast_to(code, (8, slots)).T[:, 0:1]
    best = maxima(lambda start, stop: rows_ref[start:stop], code, code_down)
    me = lax.axis_index("shard")
    for block in range(owners):
        base = block * capacity // LANES * LANES
        out_ref[me ^ block] = best[:, base:base + LANES]


def match_kernel(owners, capacity, in_ref, out_ref):
    width = in_ref.shape[1] - LANES
    meta = in_ref[:, width:]
    pick = onehots(iota((8, LANES), 0) == iota((8, LANES), 1))
    across = matmul_nt(pick, meta)
    code = across[0:1] * SPAN + across[1:2] * RADIX + across[2:3]
    down = meta.astype(jnp.float32)
    code_down = down[:, 0:1] * SPAN + down[:, 1:2] * RADIX + down[:, 2:3]
    best = maxima(lambda start, stop: in_ref[start:stop, :width], code, code_down)
    for source in range(owners):
        base = source * capacity // LANES * LANES
        out_ref[source] = best[:, base:base + LANES]


def unpack_kernel(capacity, paired, got_ref, place_ref, out_ref):
    owners = got_ref.shape[0]
    rows = place_ref.shape[1]
    me = lax.axis_index("shard")
    place = place_ref[...]
    owner = lax.div(place, capacity)
    if paired:
        owner = owner ^ me
        lane = lax.rem(place, LANES)
    else:
        lane = lax.rem(place, capacity) + lax.rem(me * capacity, LANES)
    got = got_ref[:, 0, :]
    high = got.astype(jnp.bfloat16)
    rest = got - high.astype(jnp.float32)
    middle = rest.astype(jnp.bfloat16)
    last = (rest - middle.astype(jnp.float32)).astype(jnp.bfloat16)
    pick = onehots(iota((LANES, rows), 0) == lane)
    found = matmul(high, pick) + matmul(middle, pick) + matmul(last, pick)
    mine = iota((owners, rows), 0) == owner
    out_ref[...] = jnp.sum(jnp.where(mine, found, 0.0), axis=0, keepdims=True)


def call(kernel, sizes, shapes, *args, **kwargs):
    def body(*refs):
        kernel(*sizes, *refs)

    return pl.pallas_call(
        body,
        out_shape=shapes,
        compiler_params=pltpu.CompilerParams(vmem_limit_bytes=32 * 2**20),
        **kwargs,
    )(*args)


def swap(blocks):
    owners = len(blocks)
    return [
        lax.ppermute(block, "shard", [(d, d ^ k) for d in range(owners)]) if k else block
        for k, block in zip(block_order(owners), blocks)
    ]


def shards(embeddings, cluster_ids, priority):
    rows, width = embeddings.shape
    owners = lax.axis_size("shard")
    capacity = max(2, 2 * rows // owners)
    slots = owners * capacity
    paired = owners == 16 and capacity % 16 == 0 and LANES % capacity == 0
    sizes = (owners, capacity, paired)
    place, meta = call(
        place_kernel,
        sizes,
        (
            jax.ShapeDtypeStruct((1, rows), jnp.int32),
            jax.ShapeDtypeStruct((META, slots) if paired else (slots, LANES), jnp.float32),
        ),
        (cluster_ids * SPAN + priority).reshape(1, rows),
        cost_estimate=pl.CostEstimate(
            flops=300_000_000, bytes_accessed=100_000, transcendentals=0
        ),
    )
    found = jax.ShapeDtypeStruct((owners, 1, LANES), jnp.float32)
    if paired:
        block = jax.ShapeDtypeStruct((width // LANES * capacity + META, LANES), jnp.bfloat16)
        outgoing = call(pack_kernel, sizes, [block] * owners, embeddings, place, meta)
        best = call(
            match_paired_kernel,
            (owners, capacity),
            found,
            *swap(outgoing),
            scratch_shapes=[pltpu.VMEM((slots, width), jnp.bfloat16)],
        )
    else:
        full = width + LANES
        packed = jax.ShapeDtypeStruct((slots, full), jnp.bfloat16)
        (outgoing,) = call(pack_kernel, sizes, [packed], embeddings, place, meta)
        arrived = lax.all_to_all(
            outgoing.reshape(owners, capacity, full), "shard", 0, 0, tiled=True
        ).reshape(slots, full)
        best = call(match_kernel, (owners, capacity), found, arrived)
    returned = lax.all_to_all(best, "shard", 0, 0, tiled=True)
    out = call(
        unpack_kernel,
        (capacity, paired),
        jax.ShapeDtypeStruct((1, rows), jnp.float32),
        returned,
        place,
    )
    return out.reshape(rows)


def solution(mesh):
    placed = (P(("groups", "shard"), None), P(("groups", "shard")), P(("groups", "shard")))
    return jax.shard_map(
        shards, mesh=mesh, in_specs=placed, out_specs=P(("groups", "shard")), check_vma=False
    )
```

```python
import jax
import jax.numpy as jnp
from jax import lax
from jax.experimental import pallas as pl
from jax.experimental.pallas import tpu as pltpu
from jax.sharding import PartitionSpec as P

CL_DEV = 8
LANES = 128
RADIX = 256
SPAN = 65536
META = 8


def iota(shape, dim):
    return lax.broadcasted_iota(jnp.int32, shape, dim)


def matmul_nt(left, right):
    return lax.dot_general(
        left, right, (((1,), (1,)), ((), ())), preferred_element_type=jnp.float32
    )


def matmul(left, right):
    return jnp.dot(left, right, preferred_element_type=jnp.float32)


def onehots(mask):
    return jnp.where(mask, 1.0, 0.0).astype(jnp.bfloat16)


def block_order(owners):
    half = owners // 2
    quarter = half // 2
    far = [half + part * quarter + k for k in range(quarter) for part in range(2)]
    near = list(range(half - 1, -1, -1))
    order = far[:1]
    for block in far[1:half - 1]:
        order += [near.pop(0), block]
    return order + far[half - 1:] + near


def place_kernel(owners, capacity, paired, code_ref, place_ref, meta_ref):
    rows = code_ref.shape[1]
    code = code_ref[...]
    cl = lax.div(code, SPAN)
    rk = lax.rem(code, SPAN)
    owner = lax.div(cl, CL_DEV)
    block = owner ^ lax.axis_index("shard") if paired else owner
    mine = iota((owners, rows), 0) == block
    earlier = onehots(iota((rows, rows), 0) < iota((rows, rows), 1))
    before = matmul(onehots(mine), earlier)
    pos = jnp.sum(jnp.where(mine, before, 0.0), axis=0, keepdims=True).astype(jnp.int32)
    place = block * capacity + pos
    place_ref[...] = place
    place = onehots(iota((owners * capacity, rows), 0) == place)
    line = iota((META if paired else LANES, rows), 0)
    meta = jnp.where(
        line == 0,
        cl - owner * CL_DEV + 1,
        jnp.where(line == 1, lax.div(rk, RADIX), jnp.where(line == 2, lax.rem(rk, RADIX), 0)),
    )
    meta = meta.astype(jnp.float32).astype(jnp.bfloat16)
    meta_ref[...] = matmul_nt(meta, place) if paired else matmul_nt(place, meta)


def pack_kernel(owners, capacity, paired, emb_ref, place_ref, meta_ref, *out_refs):
    rows, width = emb_ref.shape
    place = onehots(iota((owners * capacity, rows), 0) == place_ref[...])
    meta = meta_ref[...].astype(jnp.bfloat16)
    wide = emb_ref[...].astype(jnp.float32)
    squares = jnp.sum(wide * wide, axis=1, keepdims=True)
    unit = (wide * lax.rsqrt(squares + 1e-06)).astype(jnp.bfloat16)
    unit = matmul(place, unit).astype(jnp.bfloat16)
    if not paired:
        out_refs[0][:, :width] = unit
        out_refs[0][:, width:] = meta
        return
    pieces = width // LANES
    for block, out_ref in zip(block_order(owners), out_refs):
        top = block * capacity
        for piece in range(pieces):
            out_ref[piece * capacity:(piece + 1) * capacity] = unit[
                top:top + capacity, piece * LANES:(piece + 1) * LANES
            ]
        left = top // LANES * LANES
        out_ref[pieces * capacity:] = meta[:, left:left + LANES]


def maxima(units, code, code_down):
    slots = code.shape[1]
    low = code - lax.rem(code.astype(jnp.int32), SPAN).astype(jnp.float32)
    step = min(2 * LANES, slots)
    best = []
    for start in range(0, slots, step):
        stop = start + step
        sims = matmul_nt(units(0, slots), units(start, stop))
        seen = (code_down >= low[:, start:stop]) & (code_down < code[:, start:stop])
        best.append(jnp.max(jnp.where(seen, sims, -1.0), axis=0, keepdims=True))
    return jnp.concatenate(best, axis=1)


def match_paired_kernel(owners, capacity, *refs):
    *in_refs, out_ref, rows_ref = refs
    in_refs = dict(zip(block_order(owners), in_refs))
    slots, width = rows_ref.shape
    pieces = width // LANES
    for block, in_ref in in_refs.items():
        top = block * capacity
        for piece in range(pieces):
            rows_ref[top:top + capacity, piece * LANES:(piece + 1) * LANES] = in_ref[
                piece * capacity:(piece + 1) * capacity
            ]
    each = LANES // capacity
    part = lax.div(iota((META, LANES), 1), capacity)
    code = []
    for first in range(0, owners, each):
        meta = jnp.zeros((META, LANES), jnp.float32)
        for number in range(each):
            lines = in_refs[first + number][pieces * capacity:].astype(jnp.float32)
            meta = jnp.where(part == number, lines, meta)
        code.append(meta[0:1] * SPAN + meta[1:2] * RADIX + meta[2:3])
    code = jnp.concatenate(code, axis=1)
    code_down = jnp.broadcast_to(code, (8, slots)).T[:, 0:1]
    best = maxima(lambda start, stop: rows_ref[start:stop], code, code_down)
    me = lax.axis_index("shard")
    for block in range(owners):
        base = block * capacity // LANES * LANES
        out_ref[me ^ block] = best[:, base:base + LANES]


def match_kernel(owners, capacity, in_ref, out_ref):
    width = in_ref.shape[1] - LANES
    meta = in_ref[:, width:]
    pick = onehots(iota((8, LANES), 0) == iota((8, LANES), 1))
    across = matmul_nt(pick, meta)
    code = across[0:1] * SPAN + across[1:2] * RADIX + across[2:3]
    down = meta.astype(jnp.float32)
    code_down = down[:, 0:1] * SPAN + down[:, 1:2] * RADIX + down[:, 2:3]
    best = maxima(lambda start, stop: in_ref[start:stop, :width], code, code_down)
    for source in range(owners):
        base = source * capacity // LANES * LANES
        out_ref[source] = best[:, base:base + LANES]


def unpack_kernel(capacity, paired, got_ref, place_ref, out_ref):
    owners = got_ref.shape[0]
    rows = place_ref.shape[1]
    me = lax.axis_index("shard")
    place = place_ref[...]
    owner = lax.div(place, capacity)
    if paired:
        owner = owner ^ me
        lane = lax.rem(place, LANES)
    else:
        lane = lax.rem(place, capacity) + lax.rem(me * capacity, LANES)
    got = got_ref[:, 0, :]
    high = got.astype(jnp.bfloat16)
    rest = got - high.astype(jnp.float32)
    middle = rest.astype(jnp.bfloat16)
    last = (rest - middle.astype(jnp.float32)).astype(jnp.bfloat16)
    pick = onehots(iota((LANES, rows), 0) == lane)
    found = matmul(high, pick) + matmul(middle, pick) + matmul(last, pick)
    mine = iota((owners, rows), 0) == owner
    out_ref[...] = jnp.sum(jnp.where(mine, found, 0.0), axis=0, keepdims=True)


def call(kernel, sizes, shapes, *args, **kwargs):
    def body(*refs):
        kernel(*sizes, *refs)

    return pl.pallas_call(
        body,
        out_shape=shapes,
        compiler_params=pltpu.CompilerParams(vmem_limit_bytes=32 * 2**20),
        **kwargs,
    )(*args)


def swap(blocks):
    owners = len(blocks)
    return [
        lax.ppermute(block, "shard", [(d, d ^ k) for d in range(owners)]) if k else block
        for k, block in zip(block_order(owners), blocks)
    ]


def shards(embeddings, cluster_ids, priority):
    rows, width = embeddings.shape
    owners = lax.axis_size("shard")
    capacity = max(2, 2 * rows // owners)
    slots = owners * capacity
    paired = owners == 16 and capacity % 16 == 0 and LANES % capacity == 0
    sizes = (owners, capacity, paired)
    place, meta = call(
        place_kernel,
        sizes,
        (
            jax.ShapeDtypeStruct((1, rows), jnp.int32),
            jax.ShapeDtypeStruct((META, slots) if paired else (slots, LANES), jnp.float32),
        ),
        (cluster_ids * SPAN + priority).reshape(1, rows),
        cost_estimate=pl.CostEstimate(
            flops=300_000_000, bytes_accessed=100_000, transcendentals=0
        ),
    )
    found = jax.ShapeDtypeStruct((owners, 1, LANES), jnp.float32)
    if paired:
        block = jax.ShapeDtypeStruct((width // LANES * capacity + META, LANES), jnp.bfloat16)
        outgoing = call(pack_kernel, sizes, [block] * owners, embeddings, place, meta)
        best = call(
            match_paired_kernel,
            (owners, capacity),
            found,
            *swap(outgoing),
            scratch_shapes=[pltpu.VMEM((slots, width), jnp.bfloat16)],
        )
    else:
        full = width + LANES
        packed = jax.ShapeDtypeStruct((slots, full), jnp.bfloat16)
        (outgoing,) = call(pack_kernel, sizes, [packed], embeddings, place, meta)
        arrived = lax.all_to_all(
            outgoing.reshape(owners, capacity, full), "shard", 0, 0, tiled=True
        ).reshape(slots, full)
        best = call(match_kernel, (owners, capacity), found, arrived)
    returned = lax.all_to_all(best, "shard", 0, 0, tiled=True)
    out = call(
        unpack_kernel,
        (capacity, paired),
        jax.ShapeDtypeStruct((1, rows), jnp.float32),
        returned,
        place,
    )
    return out.reshape(rows)


def solution(mesh):
    placed = (P(("groups", "shard"), None), P(("groups", "shard")), P(("groups", "shard")))
    return jax.shard_map(
        shards, mesh=mesh, in_specs=placed, out_specs=P(("groups", "shard")), check_vma=False
    )
```

```python
import jax
import jax.numpy as jnp
from jax import lax
from jax.experimental import pallas as pl
from jax.experimental.pallas import tpu as pltpu
from jax.sharding import PartitionSpec as P

CL_DEV = 8
LANES = 128
RADIX = 256
SPAN = 65536
META = 8


def iota(shape, dim):
    return lax.broadcasted_iota(jnp.int32, shape, dim)


def matmul_nt(left, right):
    return lax.dot_general(
        left, right, (((1,), (1,)), ((), ())), preferred_element_type=jnp.float32
    )


def matmul(left, right):
    return jnp.dot(left, right, preferred_element_type=jnp.float32)


def onehots(mask):
    return jnp.where(mask, 1.0, 0.0).astype(jnp.bfloat16)


def block_order(owners):
    half = owners // 2
    quarter = half // 2
    near_far = [(k, k ^ 1 | quarter) for k in (*range(0, quarter, 2), *range(1, quarter, 2))]
    far = [half + distance for both in near_far for distance in both]
    near = list(range(half - 1, -1, -1))
    order = far[:2]
    for block in far[2:]:
        order += [near.pop(0), block]
    return order + near


def place_kernel(owners, capacity, paired, code_ref, place_ref, meta_ref):
    rows = code_ref.shape[1]
    code = code_ref[...]
    cl = lax.div(code, SPAN)
    rk = lax.rem(code, SPAN)
    owner = lax.div(cl, CL_DEV)
    block = owner ^ lax.axis_index("shard") if paired else owner
    mine = iota((owners, rows), 0) == block
    earlier = onehots(iota((rows, rows), 0) < iota((rows, rows), 1))
    before = matmul(onehots(mine), earlier)
    pos = jnp.sum(jnp.where(mine, before, 0.0), axis=0, keepdims=True).astype(jnp.int32)
    place = block * capacity + pos
    place_ref[...] = place
    place = onehots(iota((owners * capacity, rows), 0) == place)
    line = iota((META if paired else LANES, rows), 0)
    meta = jnp.where(
        line == 0,
        cl - owner * CL_DEV + 1,
        jnp.where(line == 1, lax.div(rk, RADIX), jnp.where(line == 2, lax.rem(rk, RADIX), 0)),
    )
    meta = meta.astype(jnp.float32).astype(jnp.bfloat16)
    meta_ref[...] = matmul_nt(meta, place) if paired else matmul_nt(place, meta)


def pack_kernel(owners, capacity, paired, emb_ref, place_ref, meta_ref, *out_refs):
    rows, width = emb_ref.shape
    place = onehots(iota((owners * capacity, rows), 0) == place_ref[...])
    meta = meta_ref[...].astype(jnp.bfloat16)
    wide = emb_ref[...].astype(jnp.float32)
    squares = jnp.sum(wide * wide, axis=1, keepdims=True)
    unit = (wide * lax.rsqrt(squares + 1e-06)).astype(jnp.bfloat16)
    unit = matmul(place, unit).astype(jnp.bfloat16)
    if not paired:
        out_refs[0][:, :width] = unit
        out_refs[0][:, width:] = meta
        return
    pieces = width // LANES
    for block, out_ref in zip(block_order(owners), out_refs):
        top = block * capacity
        for piece in range(pieces):
            out_ref[piece * capacity:(piece + 1) * capacity] = unit[
                top:top + capacity, piece * LANES:(piece + 1) * LANES
            ]
        left = top // LANES * LANES
        out_ref[pieces * capacity:] = meta[:, left:left + LANES]


def maxima(units, code, code_down):
    slots = code.shape[1]
    low = code - lax.rem(code.astype(jnp.int32), SPAN).astype(jnp.float32)
    step = min(2 * LANES, slots)
    best = []
    for start in range(0, slots, step):
        stop = start + step
        sims = matmul_nt(units(0, slots), units(start, stop))
        seen = (code_down >= low[:, start:stop]) & (code_down < code[:, start:stop])
        best.append(jnp.max(jnp.where(seen, sims, -1.0), axis=0, keepdims=True))
    return jnp.concatenate(best, axis=1)


def match_paired_kernel(owners, capacity, *refs):
    *in_refs, out_ref, rows_ref = refs
    in_refs = dict(zip(block_order(owners), in_refs))
    slots, width = rows_ref.shape
    pieces = width // LANES
    for block, in_ref in in_refs.items():
        top = block * capacity
        for piece in range(pieces):
            rows_ref[top:top + capacity, piece * LANES:(piece + 1) * LANES] = in_ref[
                piece * capacity:(piece + 1) * capacity
            ]
    each = LANES // capacity
    part = lax.div(iota((META, LANES), 1), capacity)
    code = []
    for first in range(0, owners, each):
        meta = jnp.zeros((META, LANES), jnp.float32)
        for number in range(each):
            lines = in_refs[first + number][pieces * capacity:].astype(jnp.float32)
            meta = jnp.where(part == number, lines, meta)
        code.append(meta[0:1] * SPAN + meta[1:2] * RADIX + meta[2:3])
    code = jnp.concatenate(code, axis=1)
    code_down = jnp.broadcast_to(code, (8, slots)).T[:, 0:1]
    best = maxima(lambda start, stop: rows_ref[start:stop], code, code_down)
    me = lax.axis_index("shard")
    for block in range(owners):
        base = block * capacity // LANES * LANES
        out_ref[me ^ block] = best[:, base:base + LANES]


def match_kernel(owners, capacity, in_ref, out_ref):
    width = in_ref.shape[1] - LANES
    meta = in_ref[:, width:]
    pick = onehots(iota((8, LANES), 0) == iota((8, LANES), 1))
    across = matmul_nt(pick, meta)
    code = across[0:1] * SPAN + across[1:2] * RADIX + across[2:3]
    down = meta.astype(jnp.float32)
    code_down = down[:, 0:1] * SPAN + down[:, 1:2] * RADIX + down[:, 2:3]
    best = maxima(lambda start, stop: in_ref[start:stop, :width], code, code_down)
    for source in range(owners):
        base = source * capacity // LANES * LANES
        out_ref[source] = best[:, base:base + LANES]


def unpack_kernel(capacity, paired, got_ref, place_ref, out_ref):
    owners = got_ref.shape[0]
    rows = place_ref.shape[1]
    me = lax.axis_index("shard")
    place = place_ref[...]
    owner = lax.div(place, capacity)
    if paired:
        owner = owner ^ me
        lane = lax.rem(place, LANES)
    else:
        lane = lax.rem(place, capacity) + lax.rem(me * capacity, LANES)
    got = got_ref[:, 0, :]
    high = got.astype(jnp.bfloat16)
    rest = got - high.astype(jnp.float32)
    middle = rest.astype(jnp.bfloat16)
    last = (rest - middle.astype(jnp.float32)).astype(jnp.bfloat16)
    pick = onehots(iota((LANES, rows), 0) == lane)
    found = matmul(high, pick) + matmul(middle, pick) + matmul(last, pick)
    mine = iota((owners, rows), 0) == owner
    out_ref[...] = jnp.sum(jnp.where(mine, found, 0.0), axis=0, keepdims=True)


def call(kernel, sizes, shapes, *args, **kwargs):
    def body(*refs):
        kernel(*sizes, *refs)

    return pl.pallas_call(
        body,
        out_shape=shapes,
        compiler_params=pltpu.CompilerParams(vmem_limit_bytes=32 * 2**20),
        **kwargs,
    )(*args)


def swap(blocks):
    owners = len(blocks)
    return [
        lax.ppermute(block, "shard", [(d, d ^ k) for d in range(owners)]) if k else block
        for k, block in zip(block_order(owners), blocks)
    ]


def shards(embeddings, cluster_ids, priority):
    rows, width = embeddings.shape
    owners = lax.axis_size("shard")
    capacity = max(2, 2 * rows // owners)
    slots = owners * capacity
    paired = owners == 16 and capacity % 16 == 0 and LANES % capacity == 0
    sizes = (owners, capacity, paired)
    place, meta = call(
        place_kernel,
        sizes,
        (
            jax.ShapeDtypeStruct((1, rows), jnp.int32),
            jax.ShapeDtypeStruct((META, slots) if paired else (slots, LANES), jnp.float32),
        ),
        (cluster_ids * SPAN + priority).reshape(1, rows),
        cost_estimate=pl.CostEstimate(
            flops=300_000_000, bytes_accessed=100_000, transcendentals=0
        ),
    )
    found = jax.ShapeDtypeStruct((owners, 1, LANES), jnp.float32)
    if paired:
        block = jax.ShapeDtypeStruct((width // LANES * capacity + META, LANES), jnp.bfloat16)
        outgoing = call(pack_kernel, sizes, [block] * owners, embeddings, place, meta)
        best = call(
            match_paired_kernel,
            (owners, capacity),
            found,
            *swap(outgoing),
            scratch_shapes=[pltpu.VMEM((slots, width), jnp.bfloat16)],
        )
    else:
        full = width + LANES
        packed = jax.ShapeDtypeStruct((slots, full), jnp.bfloat16)
        (outgoing,) = call(pack_kernel, sizes, [packed], embeddings, place, meta)
        arrived = lax.all_to_all(
            outgoing.reshape(owners, capacity, full), "shard", 0, 0, tiled=True
        ).reshape(slots, full)
        best = call(match_kernel, (owners, capacity), found, arrived)
    returned = lax.all_to_all(best, "shard", 0, 0, tiled=True)
    out = call(
        unpack_kernel,
        (capacity, paired),
        jax.ShapeDtypeStruct((1, rows), jnp.float32),
        returned,
        place,
    )
    return out.reshape(rows)


def solution(mesh):
    placed = (P(("groups", "shard"), None), P(("groups", "shard")), P(("groups", "shard")))
    return jax.shard_map(
        shards, mesh=mesh, in_specs=placed, out_specs=P(("groups", "shard")), check_vma=False
    )
```

```python
import jax
import jax.numpy as jnp
from jax import lax
from jax.experimental import pallas as pl
from jax.experimental.pallas import tpu as pltpu
from jax.sharding import PartitionSpec as P

CL_DEV = 8
LANES = 128
RADIX = 256
SPAN = 65536
META = 8


def iota(shape, dim):
    return lax.broadcasted_iota(jnp.int32, shape, dim)


def matmul_nt(left, right):
    return lax.dot_general(
        left, right, (((1,), (1,)), ((), ())), preferred_element_type=jnp.float32
    )


def matmul(left, right):
    return jnp.dot(left, right, preferred_element_type=jnp.float32)


def onehots(mask):
    return jnp.where(mask, 1.0, 0.0).astype(jnp.bfloat16)


def block_order(owners):
    half = owners // 2
    quarter = half // 2
    far = [half + part * quarter + k for k in range(quarter) for part in range(2)]
    near = [*range(2, half), 1, 0]
    order = far[:2]
    for block in far[2:]:
        order += [near.pop(0), block]
    return order + near


def place_kernel(owners, capacity, paired, code_ref, place_ref, meta_ref):
    rows = code_ref.shape[1]
    code = code_ref[...]
    cl = lax.div(code, SPAN)
    rk = lax.rem(code, SPAN)
    owner = lax.div(cl, CL_DEV)
    block = owner ^ lax.axis_index("shard") if paired else owner
    mine = iota((owners, rows), 0) == block
    earlier = onehots(iota((rows, rows), 0) < iota((rows, rows), 1))
    before = matmul(onehots(mine), earlier)
    pos = jnp.sum(jnp.where(mine, before, 0.0), axis=0, keepdims=True).astype(jnp.int32)
    place = block * capacity + pos
    place_ref[...] = place
    place = onehots(iota((owners * capacity, rows), 0) == place)
    line = iota((META if paired else LANES, rows), 0)
    meta = jnp.where(
        line == 0,
        cl - owner * CL_DEV + 1,
        jnp.where(line == 1, lax.div(rk, RADIX), jnp.where(line == 2, lax.rem(rk, RADIX), 0)),
    )
    meta = meta.astype(jnp.float32).astype(jnp.bfloat16)
    meta_ref[...] = matmul_nt(meta, place) if paired else matmul_nt(place, meta)


def pack_kernel(owners, capacity, paired, emb_ref, place_ref, meta_ref, *out_refs):
    rows, width = emb_ref.shape
    place = onehots(iota((owners * capacity, rows), 0) == place_ref[...])
    meta = meta_ref[...].astype(jnp.bfloat16)
    wide = emb_ref[...].astype(jnp.float32)
    squares = jnp.sum(wide * wide, axis=1, keepdims=True)
    unit = (wide * lax.rsqrt(squares + 1e-06)).astype(jnp.bfloat16)
    unit = matmul(place, unit).astype(jnp.bfloat16)
    if not paired:
        out_refs[0][:, :width] = unit
        out_refs[0][:, width:] = meta
        return
    pieces = width // LANES
    for block, out_ref in zip(block_order(owners), out_refs):
        top = block * capacity
        for piece in range(pieces):
            out_ref[piece * capacity:(piece + 1) * capacity] = unit[
                top:top + capacity, piece * LANES:(piece + 1) * LANES
            ]
        left = top // LANES * LANES
        out_ref[pieces * capacity:] = meta[:, left:left + LANES]


def maxima(units, code, code_down):
    slots = code.shape[1]
    low = code - lax.rem(code.astype(jnp.int32), SPAN).astype(jnp.float32)
    step = min(2 * LANES, slots)
    best = []
    for start in range(0, slots, step):
        stop = start + step
        sims = matmul_nt(units(0, slots), units(start, stop))
        seen = (code_down >= low[:, start:stop]) & (code_down < code[:, start:stop])
        best.append(jnp.max(jnp.where(seen, sims, -1.0), axis=0, keepdims=True))
    return jnp.concatenate(best, axis=1)


def match_paired_kernel(owners, capacity, *refs):
    *in_refs, out_ref, rows_ref = refs
    in_refs = dict(zip(block_order(owners), in_refs))
    slots, width = rows_ref.shape
    pieces = width // LANES
    for block, in_ref in in_refs.items():
        top = block * capacity
        for piece in range(pieces):
            rows_ref[top:top + capacity, piece * LANES:(piece + 1) * LANES] = in_ref[
                piece * capacity:(piece + 1) * capacity
            ]
    each = LANES // capacity
    part = lax.div(iota((META, LANES), 1), capacity)
    code = []
    for first in range(0, owners, each):
        meta = jnp.zeros((META, LANES), jnp.float32)
        for number in range(each):
            lines = in_refs[first + number][pieces * capacity:].astype(jnp.float32)
            meta = jnp.where(part == number, lines, meta)
        code.append(meta[0:1] * SPAN + meta[1:2] * RADIX + meta[2:3])
    code = jnp.concatenate(code, axis=1)
    code_down = jnp.broadcast_to(code, (8, slots)).T[:, 0:1]
    best = maxima(lambda start, stop: rows_ref[start:stop], code, code_down)
    me = lax.axis_index("shard")
    for block in range(owners):
        base = block * capacity // LANES * LANES
        out_ref[me ^ block] = best[:, base:base + LANES]


def match_kernel(owners, capacity, in_ref, out_ref):
    width = in_ref.shape[1] - LANES
    meta = in_ref[:, width:]
    pick = onehots(iota((8, LANES), 0) == iota((8, LANES), 1))
    across = matmul_nt(pick, meta)
    code = across[0:1] * SPAN + across[1:2] * RADIX + across[2:3]
    down = meta.astype(jnp.float32)
    code_down = down[:, 0:1] * SPAN + down[:, 1:2] * RADIX + down[:, 2:3]
    best = maxima(lambda start, stop: in_ref[start:stop, :width], code, code_down)
    for source in range(owners):
        base = source * capacity // LANES * LANES
        out_ref[source] = best[:, base:base + LANES]


def unpack_kernel(capacity, paired, got_ref, place_ref, out_ref):
    owners = got_ref.shape[0]
    rows = place_ref.shape[1]
    me = lax.axis_index("shard")
    place = place_ref[...]
    owner = lax.div(place, capacity)
    if paired:
        owner = owner ^ me
        lane = lax.rem(place, LANES)
    else:
        lane = lax.rem(place, capacity) + lax.rem(me * capacity, LANES)
    got = got_ref[:, 0, :]
    high = got.astype(jnp.bfloat16)
    rest = got - high.astype(jnp.float32)
    middle = rest.astype(jnp.bfloat16)
    last = (rest - middle.astype(jnp.float32)).astype(jnp.bfloat16)
    pick = onehots(iota((LANES, rows), 0) == lane)
    found = matmul(high, pick) + matmul(middle, pick) + matmul(last, pick)
    mine = iota((owners, rows), 0) == owner
    out_ref[...] = jnp.sum(jnp.where(mine, found, 0.0), axis=0, keepdims=True)


def call(kernel, sizes, shapes, *args, **kwargs):
    def body(*refs):
        kernel(*sizes, *refs)

    return pl.pallas_call(
        body,
        out_shape=shapes,
        compiler_params=pltpu.CompilerParams(vmem_limit_bytes=32 * 2**20),
        **kwargs,
    )(*args)


def swap(blocks):
    owners = len(blocks)
    return [
        lax.ppermute(block, "shard", [(d, d ^ k) for d in range(owners)]) if k else block
        for k, block in zip(block_order(owners), blocks)
    ]


def shards(embeddings, cluster_ids, priority):
    rows, width = embeddings.shape
    owners = lax.axis_size("shard")
    capacity = max(2, 2 * rows // owners)
    slots = owners * capacity
    paired = owners == 16 and capacity % 16 == 0 and LANES % capacity == 0
    sizes = (owners, capacity, paired)
    place, meta = call(
        place_kernel,
        sizes,
        (
            jax.ShapeDtypeStruct((1, rows), jnp.int32),
            jax.ShapeDtypeStruct((META, slots) if paired else (slots, LANES), jnp.float32),
        ),
        (cluster_ids * SPAN + priority).reshape(1, rows),
        cost_estimate=pl.CostEstimate(
            flops=300_000_000, bytes_accessed=100_000, transcendentals=0
        ),
    )
    found = jax.ShapeDtypeStruct((owners, 1, LANES), jnp.float32)
    if paired:
        block = jax.ShapeDtypeStruct((width // LANES * capacity + META, LANES), jnp.bfloat16)
        outgoing = call(pack_kernel, sizes, [block] * owners, embeddings, place, meta)
        best = call(
            match_paired_kernel,
            (owners, capacity),
            found,
            *swap(outgoing),
            scratch_shapes=[pltpu.VMEM((slots, width), jnp.bfloat16)],
        )
    else:
        full = width + LANES
        packed = jax.ShapeDtypeStruct((slots, full), jnp.bfloat16)
        (outgoing,) = call(pack_kernel, sizes, [packed], embeddings, place, meta)
        arrived = lax.all_to_all(
            outgoing.reshape(owners, capacity, full), "shard", 0, 0, tiled=True
        ).reshape(slots, full)
        best = call(match_kernel, (owners, capacity), found, arrived)
    returned = lax.all_to_all(best, "shard", 0, 0, tiled=True)
    out = call(
        unpack_kernel,
        (capacity, paired),
        jax.ShapeDtypeStruct((1, rows), jnp.float32),
        returned,
        place,
    )
    return out.reshape(rows)


def solution(mesh):
    placed = (P(("groups", "shard"), None), P(("groups", "shard")), P(("groups", "shard")))
    return jax.shard_map(
        shards, mesh=mesh, in_specs=placed, out_specs=P(("groups", "shard")), check_vma=False
    )
```
